32 devices in a mesh: dp: 8 (over y, x, core), tensor: 4 (over z).
Axes of the slice: x: 2, y: 2, z: 4, core: 2. Of those that a mesh axis runs over, the one named last changes fastest.
Arguments:
- inputs: bfloat16 [13848, 1024], P('dp', 'tensor'), may hold values from -12 to 12
- cotangent: bfloat16 [13848, 1024], P('dp', 'tensor'), may hold values from -6 to 6
- attn_weights: float32 [1024, 4, 1024], P('dp', None, 'tensor'), may hold values from -4 to 4
- mlp_weights: float32 [1024, 2, 4096], P('dp', None, 'tensor'), may hold values from -1 to 1
- vectors: float32 [12, 1024], replicated, may hold values from -3 to 3
- attn_mean: float32 [1024, 4, 1024], P('dp', None, 'tensor'), may hold values from -2 to 2
- mlp_mean: float32 [1024, 2, 4096], P('dp', None, 'tensor'), may hold values from -2 to 2
- vector_mean: float32 [12, 1024], replicated, may hold values from -2 to 2
- attn_square: float32 [1024, 4, 1024], P('dp', None, 'tensor'), may hold values from 0 to 1, as said below
- mlp_square: float32 [1024, 2, 4096], P('dp', None, 'tensor'), may hold values from 0 to 1, as said below
- vector_square: float32 [12, 1024], replicated, may hold values from 0 to 1, as said below
Outputs:
- output: bfloat16 [13848, 1024], P('dp', 'tensor')
- input_grad: float32 [13848, 1024], P('dp', 'tensor')
- grad_norm: float32 [], replicated
- updated_attn: float32 [1024, 4, 1024], P('dp', None, 'tensor')
- updated_mlp: float32 [1024, 2, 4096], P('dp', None, 'tensor')
- updated_vectors: float32 [12, 1024], replicated
- next_attn_mean: float32 [1024, 4, 1024], P('dp', None, 'tensor')
- next_mlp_mean: float32 [1024, 2, 4096], P('dp', None, 'tensor')
- next_vector_mean: float32 [12, 1024], replicated
- next_attn_square: float32 [1024, 4, 1024], P('dp', None, 'tensor')
- next_mlp_square: float32 [1024, 2, 4096], P('dp', None, 'tensor')
- next_vector_square: float32 [12, 1024], replicated
The draws below stay inside these ranges and needn't reach their ends.
Inputs may be any that keep to these rules, and one draw needn't show every extreme that they name: `attn_square`: entries are positive. `mlp_square`: entries are positive. `vector_square`: entries are positive.
All inputs are finite; a program needn't handle non-finite values.
Results may differ from the reference program's by a relative error of at most 0.014.
The reference program's roundings to bfloat16 on the way count: a program that leaves them out, or rounds other values in their place, can miss the bound.
Values may be sent and summed in bfloat16 or wider, within the bound.
A program may use at most 192 MiB of HBM per device.

```python
import math
import jax
import jax.numpy as jnp
from jax import lax

D = 1024
HEADS = 16
HD = 64
FF = 4096
SEQ = 577
STEP = 10
IMAGES = 24
TOKENS = 13848
VROWS = 12


def rising(length, low_end, high_end):
    return low_end + (high_end - low_end) * jnp.arange(length, dtype=jnp.float32) / (length - 1)


def base_normal(key, array_shape):
    return jnp.clip(jax.random.normal(key, array_shape, jnp.float32), -4.0, 4.0)


def gradient_scale():
    clip_limit = 0.025 * math.sqrt(D * FF * TOKENS)
    return 0.9 * clip_limit / math.sqrt(4 * D * D + 2 * D * FF)


def mean_draw(key, array_shape):
    return base_normal(key, array_shape) * (0.11 * gradient_scale())


def square_draw(key, array_shape):
    level = gradient_scale() ** 2 / 999.0
    return jnp.exp(jax.random.uniform(key, array_shape, jnp.float32, math.log(0.7), math.log(3.0))) * level


def draw_inputs(key, part):
    key = jax.random.fold_in(key, 11)
    first_key, second_key = jax.random.split(key)
    base_draw = base_normal(first_key, (TOKENS, D))
    columns = rising(D, 0.5, 1.5)
    row_scale = jnp.exp(jax.random.uniform(second_key, (TOKENS, 1), jnp.float32, math.log(0.5), math.log(2.0)))
    return (base_draw * columns * row_scale).astype(jnp.bfloat16)


def draw_cotangent(key, part):
    key = jax.random.fold_in(key, 12)
    base_draw = base_normal(key, (TOKENS, D))
    columns = rising(D, 0.5, 1.5)
    return (base_draw * columns).astype(jnp.bfloat16)


def draw_attn_weights(key, part):
    key = jax.random.fold_in(key, 13)
    base_draw = base_normal(key, (D, 4, D))
    columns = rising(D, 0.6, 1.8)
    inner_rows = base_draw[:, :3, :] / math.sqrt(D)
    outer_rows = base_draw[:, 3:, :] * (3.0 / math.sqrt(D)) * columns
    return jnp.concatenate((inner_rows, outer_rows), axis=1)


def draw_mlp_weights(key, part):
    key = jax.random.fold_in(key, 14)
    base_draw = base_normal(key, (D, 2, FF))
    columns = rising(FF, 0.6, 1.8)
    first_rows = base_draw[:, :1, :] / math.sqrt(D)
    second_rows = base_draw[:, 1:, :] * (1.5 / math.sqrt(FF)) * columns
    return jnp.concatenate((first_rows, second_rows), axis=1)


def draw_vectors(key, part):
    key = jax.random.fold_in(key, 15)
    base_draw = base_normal(key, (VROWS, D))
    columns = rising(D, 0.6, 1.8)
    gain_one = columns * (1.0 + 0.1 * base_draw[0:1])
    gain_two = columns * (1.0 + 0.1 * base_draw[2:3])
    return jnp.concatenate((gain_one, 0.2 * base_draw[1:2], gain_two, 0.2 * base_draw[3:4], 0.3 * base_draw[4:6], 0.2 * base_draw[6:8], 0.3 * base_draw[8:]), axis=0)


def draw_attn_mean(key, part):
    key = jax.random.fold_in(key, 21)
    return mean_draw(key, (D, 4, D))


def draw_mlp_mean(key, part):
    key = jax.random.fold_in(key, 22)
    return mean_draw(key, (D, 2, FF))


def draw_vector_mean(key, part):
    key = jax.random.fold_in(key, 23)
    return mean_draw(key, (VROWS, D))


def draw_attn_square(key, part):
    key = jax.random.fold_in(key, 31)
    return square_draw(key, (D, 4, D))


def draw_mlp_square(key, part):
    key = jax.random.fold_in(key, 32)
    return square_draw(key, (D, 2, FF))


def draw_vector_square(key, part):
    key = jax.random.fold_in(key, 33)
    return square_draw(key, (VROWS, D))


def setup_inputs(seed: int = 0) -> dict:
    seeds = jax.random.split(jax.random.key(seed), 12)
    return {
        "inputs": draw_inputs(jax.random.fold_in(seeds[11], 71), 0),
        "cotangent": draw_cotangent(jax.random.fold_in(seeds[11], 71), 0),
        "attn_weights": draw_attn_weights(jax.random.fold_in(seeds[11], 71), 0),
        "mlp_weights": draw_mlp_weights(jax.random.fold_in(seeds[11], 71), 0),
        "vectors": draw_vectors(jax.random.fold_in(seeds[11], 71), 0),
        "attn_mean": draw_attn_mean(jax.random.fold_in(seeds[11], 71), 0),
        "mlp_mean": draw_mlp_mean(jax.random.fold_in(seeds[11], 71), 0),
        "vector_mean": draw_vector_mean(jax.random.fold_in(seeds[11], 71), 0),
        "attn_square": draw_attn_square(jax.random.fold_in(seeds[11], 71), 0),
        "mlp_square": draw_mlp_square(jax.random.fold_in(seeds[11], 71), 0),
        "vector_square": draw_vector_square(jax.random.fold_in(seeds[11], 71), 0),
    }


@jax.custom_vjp
def low(v):
    return lax.optimization_barrier(v.astype(jnp.bfloat16)).astype(jnp.float32)

@jax.custom_vjp
def low_back(v):
    return v

def low_keep(v):
    return (low(v), None)

def low_pass(kept, grad):
    return (grad,)

def back_keep(v):
    return (v, None)

def back_low(kept, grad):
    return (low(grad),)
low.defvjp(low_keep, low_pass)
low_back.defvjp(back_keep, back_low)
beta_one = 0.9
beta_two = 0.999
rate_matrix = 0.1
rate_vector = 0.5
decay_matrix = 0.1
adam_eps = 1e-08
norm_eps = 1e-06
clip_ratio = 0.025

def layer_norm(rows_in, gain, shift):
    center = rows_in - lax.optimization_barrier(jnp.mean(rows_in, axis=-1, keepdims=True))
    inv_std = lax.rsqrt(lax.optimization_barrier(jnp.mean(center * center, axis=-1, keepdims=True)) + norm_eps)
    return center * inv_std * gain + shift

def matmul(left, right):
    return jnp.dot(left, right, precision=lax.Precision.HIGHEST)

def attend(pieces):
    queries, key_rows, value_rows = pieces
    scores = jnp.einsum('qhe,khe->hqk', queries, key_rows, precision=lax.Precision.HIGHEST) * HD ** (-0.5)
    probs = low(jax.nn.softmax(low_back(scores), axis=-1))
    return jnp.einsum('hqk,khe->qhe', probs, value_rows, precision=lax.Precision.HIGHEST)

def forward(attn_weights, mlp_weights, vectors, inputs_f):
    attn_low = low(attn_weights)
    mlp_low = low(mlp_weights)
    ln_one = low(layer_norm(inputs_f, vectors[0], vectors[1]))
    queries = low(low_back(matmul(ln_one, attn_low[:, 0, :]) + vectors[4]))
    key_rows = low(low_back(matmul(ln_one, attn_low[:, 1, :])))
    value_rows = low(low_back(matmul(ln_one, attn_low[:, 2, :]) + vectors[5]))
    image_shape = (IMAGES, SEQ, HEADS, HD)
    mixed_heads = lax.map(jax.checkpoint(attend), (queries.reshape(image_shape), key_rows.reshape(image_shape), value_rows.reshape(image_shape)))
    mixed_heads = low(low_back(mixed_heads.reshape(TOKENS, D)))
    residual = inputs_f + low_back(matmul(mixed_heads, attn_low[:, 3, :].T)) + vectors[6]
    ln_two = low(layer_norm(residual, vectors[2], vectors[3]))
    pre_act = low_back(matmul(ln_two, mlp_low[:, 0, :]) + vectors[8:].reshape(FF))
    hidden = low(jax.nn.gelu(pre_act, approximate=False))
    return residual + matmul(hidden, mlp_low[:, 1, :].T) + vectors[7]

def adam_step(weight, grad, mean, square, rate, decay):
    next_mean = beta_one * mean + (1.0 - beta_one) * grad
    next_square = beta_two * square + (1.0 - beta_two) * grad * grad
    mean_hat = next_mean / (1.0 - beta_one ** STEP)
    square_hat = next_square / (1.0 - beta_two ** STEP)
    updated = weight - rate * (mean_hat / (jnp.sqrt(square_hat) + adam_eps) + decay * weight)
    return (updated, next_mean, next_square)

def reference(inputs, cotangent, attn_weights, mlp_weights, vectors, attn_mean, mlp_mean, vector_mean, attn_square, mlp_square, vector_square):
    inputs_f = inputs.astype(jnp.float32)
    output, pullback = jax.vjp(forward, attn_weights, mlp_weights, vectors, inputs_f)
    attn_grad, mlp_grad, vector_grad, input_grad = pullback(cotangent.astype(jnp.float32))
    squares = jnp.sum(attn_grad * attn_grad) + jnp.sum(mlp_grad * mlp_grad) + jnp.sum(vector_grad * vector_grad)
    grad_norm = jnp.sqrt(squares)
    clip_limit = clip_ratio * math.sqrt(D * FF * TOKENS)
    factor = jnp.minimum(1.0, clip_limit / (grad_norm + norm_eps))
    updated_attn, next_attn_mean, next_attn_square = adam_step(attn_weights, factor * attn_grad, attn_mean, attn_square, rate_matrix, decay_matrix)
    updated_mlp, next_mlp_mean, next_mlp_square = adam_step(mlp_weights, factor * mlp_grad, mlp_mean, mlp_square, rate_matrix, decay_matrix)
    updated_vectors, next_vector_mean, next_vector_square = adam_step(vectors, factor * vector_grad, vector_mean, vector_square, rate_vector, 0.0)
    return (output.astype(jnp.bfloat16), input_grad, grad_norm, updated_attn, updated_mlp, updated_vectors, next_attn_mean, next_mlp_mean, next_vector_mean, next_attn_square, next_mlp_square, next_vector_square)
```

```python
import math

import jax
import jax.numpy as jnp
from jax import lax
from jax.experimental import pallas as pl
from jax.experimental.pallas import tpu as pltpu
from jax.sharding import PartitionSpec as P

HD = 64
SEQ = 577
STEP = 10

beta_one = 0.9
beta_two = 0.999
rate_matrix = 0.1
rate_vector = 0.5
decay_matrix = 0.1
adam_eps = 1e-08
norm_eps = 1e-06
clip_ratio = 0.025

BF = jnp.bfloat16
F32 = jnp.float32

FULL = 592
PART = 304
HALF = SEQ // 2 + 1
OWN = FULL + PART
ALL = OWN + PART
CORE_ROWS = OWN // 2
PIECES = 4
ITEMS = 4 + 2 * PIECES
VMEM_LIMIT = 64 * 2**20
SLOTS = 5
QUERY, KEY, VALUE, OUT = range(4)
MESH = pl.DeviceIdType.MESH


def dot(left, right, dims):
    return lax.dot_general(left, right, ((dims[:1], dims[1:]), ((), ())), preferred_element_type=F32)


def xor(index, mask):
    out = index
    bit = 1
    while bit <= mask:
        if mask & bit:
            out = out + bit * (1 - 2 * ((index // bit) % 2))
        bit *= 2
    return out


def normalize(rows_in):
    center = rows_in - jnp.mean(rows_in, axis=-1, keepdims=True)
    inv_std = lax.rsqrt(jnp.mean(center * center, axis=-1, keepdims=True) + norm_eps)
    return center * inv_std, inv_std


def normalize_back(scaled, normed, inv_std):
    return inv_std * (
        scaled
        - jnp.mean(scaled, axis=-1, keepdims=True)
        - normed * jnp.mean(scaled * normed, axis=-1, keepdims=True)
    )


def gelu_parts(u):
    a = jnp.abs(u)
    t = 1.0 / (1.0 + (0.3275911 / math.sqrt(2.0)) * a)
    e = jnp.exp(-0.5 * u * u)
    poly = t * (
        0.254829592 + t * (-0.284496736 + t * (1.421413741 + t * (-1.453152027 + t * 1.061405429)))
    )
    tail = 0.5 * poly * e
    phi_big = jnp.where(u >= 0, 1.0 - tail, tail)
    return phi_big, u * e * (1.0 / math.sqrt(2.0 * math.pi))


class Place:
    def __init__(self, rows, columns):
        self.dp = lax.axis_index("dp")
        self.z = lax.axis_index("tensor")
        self.core = self.dp % 2
        self.chip = self.dp // 2
        self.chips = lax.axis_size("dp") // 2
        self.zs = lax.axis_size("tensor")
        self.core_rows = rows
        self.rows = 2 * rows
        self.columns = columns
        count = self.chips.bit_length() - 1
        fast = [1 << i for i in range((count + 1) // 2)]
        slow = [1 << i for i in range((count + 1) // 2, count)]
        self.orders = (fast + slow, slow + fast)
        self.z_bits = [1 << i for i in range(self.zs.bit_length() - 1)]

    def at(self, core=0, chip=0, z=0):
        return (xor(self.dp, core + 2 * chip), xor(self.z, z))

    def chip_rows(self, mask, count=1):
        return pl.ds(pl.multiple_of(xor(self.chip, mask) * self.rows, self.rows), count * self.rows)

    def z_columns(self, mask):
        return pl.ds(pl.multiple_of(xor(self.z, mask) * self.columns, self.columns), self.columns)

    def half_rows(self, core):
        start = self.chip * self.rows + core * self.core_rows
        return pl.ds(pl.multiple_of(start, self.core_rows), self.core_rows)


def remote(src, dst, send, recv, device):
    copy = pltpu.make_async_remote_copy(
        src_ref=src, dst_ref=dst, send_sem=send, recv_sem=recv, device_id=device, device_id_type=MESH
    )
    copy.start()
    return copy


def gather_steps(place, weight, theirs, send_sem, recv_sem):
    used = [0]

    def send(rows, columns, device, src=None):
        ref = weight.at[rows, columns]
        k = used[0]
        used[0] += 1
        return remote(ref if src is None else src, ref, send_sem.at[k], recv_sem.at[k], device)

    half = place.half_rows(place.core)
    copies = [send(half, place.z_columns(0), place.at(core=1), theirs)]
    yield
    for copy in copies:
        copy.wait()
    have = [0]
    for bit in reversed(place.z_bits):
        copies = [send(place.chip_rows(0), place.z_columns(m), place.at(z=bit)) for m in have]
        yield
        for copy in copies:
            copy.wait()
        have = have + [m ^ bit for m in have]
    width = place.zs * place.columns
    parts = (slice(0, width // 2), slice(width // 2, width))
    haves = [[0], [0]]
    for step in range(len(place.orders[0])):
        copies = []
        for i, columns in enumerate(parts):
            bit = place.orders[i][step]
            masks = sorted(haves[i])
            count = len(masks)
            if masks == list(range(count)):
                start = place.chip // count * count
                rows = pl.ds(pl.multiple_of(start * place.rows, place.rows), count * place.rows)
                copies.append(send(rows, columns, place.at(chip=bit)))
            else:
                for m in masks:
                    copies.append(send(place.chip_rows(m), columns, place.at(chip=bit)))
            haves[i] = masks + [m ^ bit for m in masks]
        yield
        for copy in copies:
            copy.wait()


def add_block(ref, rows, columns, other):
    ref[rows, columns] = (ref[rows, columns].astype(F32) + other.astype(F32)).astype(BF)


def scatter_steps(place, weight, by_rows, by_columns, final, send_sem, recv_sem):
    used = [0]

    def send(src, dst, device):
        k = used[0]
        used[0] += 1
        return remote(src, dst, send_sem.at[k], recv_sem.at[k], device)

    width = place.zs * place.columns
    parts = (slice(0, width // 2), slice(width // 2, width))
    haves = [list(range(place.chips))] * 2
    base = 0
    for step in reversed(range(len(place.orders[0]))):
        copies, adds = [], []
        bits = [order[step] for order in place.orders]
        haves = [[m for m in have if not m & bit] for have, bit in zip(haves, bits)]
        for slot in range(len(haves[0])):
            there = pl.ds(base + slot * place.rows, place.rows)
            for columns, bit, have in zip(parts, bits, haves):
                m = have[slot]
                src = weight.at[place.chip_rows(m ^ bit), columns]
                copies.append(send(src, by_rows.at[there, columns], place.at(chip=bit)))
                adds.append((place.chip_rows(m), columns, there))
        base += len(haves[0]) * place.rows
        yield
        for copy in copies:
            copy.wait()
        for rows, columns, there in adds:
            add_block(weight, rows, columns, by_rows[there, columns])
    have = list(range(place.zs))
    base = 0
    for bit in place.z_bits:
        keep = [m for m in have if not m & bit]
        copies, adds = [], []
        for slot, m in enumerate(keep):
            there = pl.ds(base + slot * place.columns, place.columns)
            src = weight.at[place.chip_rows(0), place.z_columns(m ^ bit)]
            copies.append(send(src, by_columns.at[:, there], place.at(z=bit)))
            adds.append((m, there))
        base += len(keep) * place.columns
        have = keep
        yield
        for copy in copies:
            copy.wait()
        for m, there in adds:
            add_block(weight, place.chip_rows(0), place.z_columns(m), by_columns[:, there])
    other = weight.at[place.half_rows(1 - place.core), place.z_columns(0)]
    copy = send(other, final.at[place.core], place.at(core=1))
    final[pl.ds(place.core, 1)] = weight[place.half_rows(place.core), place.z_columns(0)][None]
    yield
    copy.wait()


def sum_steps(place, value, slots, send_sem, recv_sem):
    partners = [place.at(chip=bit) for bit in place.orders[0]]
    partners += [place.at(z=bit) for bit in place.z_bits] + [place.at(core=1)]
    for k, partner in enumerate(partners):
        slots[2 * k] = value[...]
        copy = remote(slots.at[2 * k], slots.at[2 * k + 1], send_sem.at[k], recv_sem.at[k], partner)
        yield
        copy.wait()
        value[...] = slots[2 * k] + slots[2 * k + 1]


def layer_kernel(
    attn_in, mlp_in, inputs, cotangent, vec,
    output, input_grad, attn_grad, mlp_grad, vec_sum, norm_out,
    w, theirs, fin, out_got, grad_got, norm_sum, x, ln_one, q, k, v, mixed, lse, cot, ln_two, acc_out, acc_two, res, pre, gh, hid, gp,
    box, got_half, got_out, got_rest, got_pair, by_rows, by_columns,
    sums, up_sums, vec_slots, norm_slots,
    ag_send, ag_recv, rs_send, rs_recv, xs_send, xs_recv, ms_send, ms_recv, vs_send, vs_recv, ns_send, ns_recv,
):
    width = x.shape[1]
    place = Place(fin.shape[2], fin.shape[3])
    core, z = place.core, place.z
    z_low = z % 2
    z_high = z // 2


    barrier = pltpu.get_barrier_semaphore()
    for c in range(2):
        for m in range(4):
            if c or m:
                pl.semaphore_signal(barrier, inc=1, device_id=place.at(core=c, z=m), device_id_type=MESH)
    for bit in place.orders[0]:
        pl.semaphore_signal(barrier, inc=1, device_id=place.at(chip=bit), device_id_type=MESH)
    pl.semaphore_wait(barrier, 7 + len(place.orders[0]))

    gathers = [
        gather_steps(place, w.at[i], theirs.at[i], ag_send.at[i], ag_recv.at[i])
        for i in range(ITEMS)
    ]
    steps = len(place.orders[0])
    offsets = [0, 1] + [2 + 2 * s for s in range(steps + 1)]
    gather_events = sorted(
        (i + offset, -s, i) for i in range(ITEMS) for s, offset in enumerate(offsets)
    )
    gather_last = gather_events[-1][0]

    def gather_item(item):
        gather_to(item + offsets[-1])

    def gather_to(tick):
        while gather_events and gather_events[0][0] <= tick:
            next(gathers[gather_events.pop(0)[2]], None)

    scatter_order = [(i, i) for i in range(4, ITEMS)]
    scatter_order += [(OUT, OUT), (VALUE, 4), (KEY, 5), (QUERY, 6)]
    scatters = [
        scatter_steps(
            place, w.at[slot], by_rows.at[n % SLOTS], by_columns.at[n % SLOTS], fin.at[i],
            rs_send.at[i], rs_recv.at[i],
        )
        for n, (i, slot) in enumerate(scatter_order)
    ]
    scatter_offsets = [0] + [2 + s for s in range(steps + 4)]
    scatter_events = sorted(
        (n + offset, -s, n) for n in range(ITEMS) for s, offset in enumerate(scatter_offsets)
    )
    scatter_last = scatter_events[-1][0]

    def scatter_to(tick):
        while scatter_events and scatter_events[0][0] <= tick:
            next(scatters[scatter_events.pop(0)[2]], None)

    def swap(src, dst, index, device):
        return remote(src, dst, ms_send.at[index], ms_recv.at[index], device)

    stay = core == z_high

    SECTIONS = (
        (0, 304, 0, FULL + 2 * PART),
        (304, 288, 304, FULL + 2 * PART + 304),
        (FULL, PART, FULL, FULL + PART),
        (OWN, PART, FULL + PART, FULL),
    )

    def send_rows(src, dst, section, chunk):
        start, size, even, odd = SECTIONS[section]
        columns = pl.ds(pl.multiple_of(z * src.shape[1], src.shape[1]), src.shape[1])
        rows = pl.ds(start, size)
        there = dst.at[rows, columns]
        first = pl.multiple_of(even + z_low * (odd - even), 16)
        second = pl.multiple_of(odd + z_low * (even - odd), 16)
        src_same, src_cross = src.at[pl.ds(first, size), :], src.at[pl.ds(second, size), :]
        target = (2 * place.chip + z_high, 2 * core + z_low)
        other = (2 * place.chip + z_high, 2 * core + 1 - z_low)

        @pl.when(stay)
        def _():
            pltpu.make_async_copy(src_same, there, xs_recv.at[chunk, 0]).start()

        @pl.when(jnp.logical_not(stay))
        def _():
            remote(src_same, there, xs_send.at[chunk, 0], xs_recv.at[chunk, 0], target)

        copy = remote(src_cross, there, xs_send.at[chunk, 1], xs_recv.at[chunk, 1], other)

        def wait():
            whole = pltpu.make_async_remote_copy(
                src_ref=src_same, dst_ref=there, send_sem=xs_send.at[chunk, 0],
                recv_sem=xs_recv.at[chunk, 0], device_id=other, device_id_type=MESH,
            )

            @pl.when(jnp.logical_not(stay))
            def _():
                whole.wait_send()

            whole.wait_recv()
            copy.wait()

            half = width // 2
            here = dst.at[rows, pl.ds(pl.multiple_of(core * half, half), half)]
            return remote(here, here, xs_send.at[chunk, 2], xs_recv.at[chunk, 2], place.at(core=1))

        return wait

    def own_rows(size, start=0):
        return pl.ds(pl.multiple_of(core * CORE_ROWS + start, 16), size)

    def other_rows(size, start=0):
        return pl.ds(pl.multiple_of((1 - core) * CORE_ROWS + start, 16), size)

    def tiles(total, size, body):
        @pl.loop(0, total // size)
        def _(t):
            body(pl.multiple_of(t * size, size))

    def norm_rows(start):
        rows = pl.ds(start, 80)
        normed, _ = normalize(x[rows, :].astype(F32))
        ln_one[rows, :] = (normed * vec[0:1, :] + vec[1:2, :]).astype(BF)

    def head_bias(row):
        size = place.columns
        parts = []
        for i in range(place.zs):
            low = vec[row : row + 1, 2 * i * size : (2 * i + 1) * size]
            high = vec[row : row + 1, (2 * i + 1) * size : (2 * i + 2) * size]
            parts.append(jnp.where(core == 0, low, high))
        return jnp.concatenate(parts, axis=1)

    def up_bias(piece):
        size = place.columns
        parts = []
        for i in range(place.zs):
            low = vec[8 + i : 9 + i, piece * size : (piece + 1) * size]
            high = vec[8 + i : 9 + i, (PIECES + piece) * size : (PIECES + piece + 1) * size]
            parts.append(jnp.where(core == 0, low, high))
        return jnp.concatenate(parts, axis=1)

    def project(item, dst, bias):
        def body(start):
            rows = pl.ds(start, 240)
            value = dot(ln_one[rows, :], w[item], (1, 0))
            if bias is not None:
                value = value + bias
            dst[rows, :] = value.astype(BF)

        tiles(ALL, 240, body)

    IMAGES = ((0, FULL, FULL), (FULL, PART, 2 * PART))

    def masked(q_in, k_in, low):
        scores = dot(q_in, k_in, (1, 1)) * HD**-0.5
        col = lax.broadcasted_iota(jnp.int32, scores.shape, 1)
        if low:
            inside = jnp.where(col < PART, col, col - PART)
            good = (inside < HALF) & (col != PART * (1 - z_low))
        else:
            good = col < SEQ
        return jnp.where(good, scores, -1e30)

    def attend(pair):
        lanes = pl.ds(pl.multiple_of(pair * 2 * HD, 2 * HD), 2 * HD)
        for low, size, keys in IMAGES:
            q_in, k_in, v_in = q[low : low + size, lanes], k[low : low + keys, lanes], v[low : low + keys, lanes]
            outs, logs = [], []
            for head in range(2):
                cut = slice(head * HD, (head + 1) * HD)
                scores = masked(q_in[:, cut], k_in[:, cut], low)
                peaks = jnp.max(scores, axis=-1, keepdims=True)
                exponent = jnp.exp(scores - peaks)
                totals = jnp.sum(exponent, axis=-1, keepdims=True)
                probs = (exponent * (1.0 / totals)).astype(BF)
                outs.append(dot(probs, v_in[:, cut], (1, 0)))
                logs.append(jnp.broadcast_to(peaks + jnp.log(totals), (size, HD)))
            mixed[low : low + size, lanes] = jnp.concatenate(outs, axis=1).astype(BF)
            lse[low : low + size, lanes] = jnp.concatenate(logs, axis=1)

    def attend_back(pair):
        lanes = pl.ds(pl.multiple_of(pair * 2 * HD, 2 * HD), 2 * HD)
        scale = HD**-0.5
        for low, size, keys in IMAGES:
            q_in, k_in, v_in = q[low : low + size, lanes], k[low : low + keys, lanes], v[low : low + keys, lanes]
            do_in, o_in = hid[low : low + size, lanes], mixed[low : low + size, lanes]
            logs = lse[low : low + size, lanes]
            dqs, dks, dvs = [], [], []
            for head in range(2):
                cut = slice(head * HD, (head + 1) * HD)
                do = do_in[:, cut]
                scores = masked(q_in[:, cut], k_in[:, cut], low)
                probs = jnp.exp(scores - logs[:, head * HD : head * HD + 1])
                grad_probs = dot(do, v_in[:, cut], (1, 1))
                delta = jnp.sum(do.astype(F32) * o_in[:, cut].astype(F32), axis=-1, keepdims=True)
                ds = (probs * (grad_probs - delta)).astype(BF)
                dqs.append(dot(ds, k_in[:, cut], (1, 0)) * scale)
                dks.append(dot(ds, q_in[:, cut], (0, 0)) * scale)
                dvs.append(dot(probs.astype(BF), do, (0, 0)))
            q[low : low + size, lanes] = jnp.concatenate(dqs, axis=1).astype(BF)
            k[low : low + keys, lanes] = jnp.concatenate(dks, axis=1).astype(BF)
            v[low : low + keys, lanes] = jnp.concatenate(dvs, axis=1).astype(BF)

    def row_sum(value):
        return jnp.sum(value.reshape(-1, 8, value.shape[-1]), axis=0)

    for i in range(ITEMS):
        if i < 4:
            low, high = (attn_in[:, i, h * place.columns : (h + 1) * place.columns] for h in range(2))
        else:
            piece, which = (i - 4) // 2, i % 2
            at = [(h * PIECES + piece) * place.columns for h in range(2)]
            low, high = (mlp_in[:, which, t : t + place.columns] for t in at)
        low, high = low.astype(BF), high.astype(BF)
        w[i, place.half_rows(core), place.z_columns(0)] = jnp.where(core == 0, low, high)
        theirs[i] = jnp.where(core == 0, high, low)

    def split_rows(src, dst):
        middle, last = SEQ + HALF, 2 * SEQ
        whole = input_grad
        whole[...] = src[...].astype(F32)
        gap = jnp.zeros((FULL - SEQ, src.shape[1]), F32)
        dst[0:FULL, :] = jnp.concatenate((whole[0:SEQ, :], gap)).astype(BF)
        dst[FULL:OWN, :] = jnp.concatenate((whole[SEQ:middle, :], gap)).astype(BF)
        upper = jnp.concatenate((gap[0:1], whole[middle:last, :], gap))
        dst[OWN:ALL, :] = upper.astype(BF)
        dst[ALL:, :] = jnp.concatenate((whole[last:, :], gap)).astype(BF)

    for i in range(ITEMS):
        next(gathers[i])
    split_rows(inputs, out_got)
    gather_to(2)
    waits, swaps = [], []
    ready = 0
    for chunk in range(4):
        if chunk:
            swaps.append(waits[-1]())
        waits.append(send_rows(out_got, x, chunk, chunk))
        gather_to(3 + chunk)
        if chunk > 1:
            swaps[chunk - 2].wait()
            while ready + 80 <= SECTIONS[chunk - 2][0] + SECTIONS[chunk - 2][1]:
                norm_rows(ready)
                ready += 80
    swaps.append(waits[-1]())
    cot_waits, cot_swaps = [], []

    def send_cot(chunk):
        cot_waits.append(send_rows(grad_got, cot, chunk, 4 + chunk))

    split_rows(cotangent, grad_got)
    send_cot(0)
    for swap_x in swaps[2:]:
        swap_x.wait()

    def norm_more(start):
        norm_rows(pl.multiple_of(ready + start, 16))

    tiles(ALL - ready, 80, norm_more)
    gather_item(QUERY)
    project(QUERY, q, head_bias(4))
    gather_to(8)
    send_cot(1)
    gather_item(KEY)
    project(KEY, k, None)
    gather_item(VALUE)
    project(VALUE, v, head_bias(5))
    for pair in range(4):
        attend(pair)
        if pair == 1:
            gather_item(OUT)
            cot_swaps.append(cot_waits[0]())
            send_cot(2)
        if pair == 3:
            gather_to(10)
            cot_swaps.append(cot_waits[1]())

    def out_other(start):
        rows = other_rows(224, start)
        box[pl.ds(start, 224), :] = dot(mixed[rows, :], w[OUT], (1, 1)).astype(BF)

    tiles(CORE_ROWS, 224, out_other)
    copy_attn = swap(box, got_half, 6, place.at(core=1))

    def out_own(start):
        rows = own_rows(224, start)
        value = dot(mixed[rows, :], w[OUT], (1, 1))
        res[pl.ds(start, 224), :] = value + x[rows, :].astype(F32) + vec[6:7, :]

    tiles(CORE_ROWS, 224, out_own)
    copy_attn.wait()

    def norm_two(start):
        rows = pl.ds(start, 32)
        value = res[rows, :] + got_half[rows, :].astype(F32)
        res[rows, :] = value
        normed, _ = normalize(value)
        ln_two[own_rows(32, start), :] = (normed * vec[2:3, :] + vec[3:4, :]).astype(BF)

    tiles(CORE_ROWS, 32, norm_two)
    mine_two = ln_two.at[own_rows(CORE_ROWS), :]
    copy_two = swap(mine_two, mine_two, 7, place.at(core=1))
    gather_item(5)
    cot_swaps.append(cot_waits[2]())
    for copy in cot_swaps:
        copy.wait()
    copy_two.wait()

    up_sums[...] = jnp.zeros_like(up_sums)

    def mlp_piece(piece, hook):
        up, down = 4 + 2 * piece, 5 + 2 * piece
        gather_item(down)
        bias = up_bias(piece)

        def rows_part(start):
            rows = pl.ds(start, CORE_ROWS)
            pre[...] = dot(ln_two[rows, :], w[up], (1, 0))
            gh[...] = dot(cot[rows, :], w[down], (1, 0))

            def activate(at):
                inside = pl.ds(at, 16)
                u = pre[inside, :] + bias
                cdf, slope = gelu_parts(u)
                grad = (gh[inside, :] * (cdf + slope)).astype(BF)
                hid[pl.ds(start + at, 16), :] = (u * cdf).astype(BF)
                gp[pl.ds(start + at, 16), :] = grad
                up_sums[piece] += row_sum(grad.astype(F32))

            tiles(CORE_ROWS, 16, activate)
            out = dot(hid[rows, :], w[down], (1, 1))
            two = dot(gp[rows, :], w[up], (1, 1))
            if piece:
                acc_out[rows, :] += out
                acc_two[rows, :] += two
            else:
                acc_out[rows, :] = out
                acc_two[rows, :] = two

        tiles(OWN, CORE_ROWS, rows_part)
        hook()

        def up_rows(start):
            rows = pl.ds(start, 256)
            w[up, rows, :] = dot(ln_two[:, rows], gp[...], (0, 0)).astype(BF)
            w[down, rows, :] = dot(cot[:, rows], hid[...], (0, 0)).astype(BF)

        tiles(width, 256, up_rows)

    def nothing():
        pass

    early = gather_last - 2 * PIECES
    mlp_piece(0, nothing)
    gather_to(early + 4)
    mlp_piece(1, lambda: gather_to(early + 5))
    scatter_to(0)
    gather_to(early + 6)
    scatter_to(1)
    mlp_piece(2, lambda: gather_to(early + 7))
    scatter_to(2)
    gather_to(gather_last)
    scatter_to(3)
    mlp_piece(3, lambda: scatter_to(4))

    def send_half(acc, start):
        box[pl.ds(start, 64), :] = acc[other_rows(64, start), :].astype(BF)

    tiles(CORE_ROWS, 64, lambda start: send_half(acc_two, start))
    copy_two = swap(box, got_half, 8, place.at(core=1))
    sums[...] = jnp.zeros_like(sums)
    copy_two.wait()

    def back_two(start):
        rows, held = pl.ds(start, 32), own_rows(32, start)
        normed, inv_std = normalize(res[rows, :])
        grad = acc_two[held, :] + got_half[rows, :].astype(F32)
        grad_out = cot[held, :].astype(F32)
        acc_two[held, :] = grad_out + normalize_back(grad * vec[2:3, :], normed, inv_std)
        sums[2] += row_sum(grad * normed)
        sums[3] += row_sum(grad)
        sums[6] += row_sum(acc_two[held, :])
        sums[7] += row_sum(grad_out)
        ln_two[held, :] = acc_two[held, :].astype(BF)

    tiles(CORE_ROWS, 32, back_two)
    mine_two = ln_two.at[own_rows(CORE_ROWS), :]
    copy_grad = swap(mine_two, mine_two, 9, place.at(core=1))
    tiles(CORE_ROWS, 64, lambda start: send_half(acc_out, start))
    copy_out = swap(box, got_out, 10, place.at(core=1))
    copy_grad.wait()

    def grad_heads(start):
        rows = pl.ds(start, CORE_ROWS)
        hid[rows, :] = dot(ln_two[rows, :], w[OUT], (1, 0)).astype(BF)

    tiles(OWN, CORE_ROWS, grad_heads)

    def weight_grad(item, left, size, right):
        def body(start):
            rows = pl.ds(start, 256)
            w[item, rows, :] = dot(left[0:size, rows], right[0:size, :], (0, 0)).astype(BF)

        tiles(width, 256, body)

    scatter_to(5)
    copy_out.wait()

    def got_rows(got, slot):
        return got.at[pl.ds(pl.multiple_of(slot * CORE_ROWS, CORE_ROWS), CORE_ROWS), :]

    def send_out(got, index):
        copies = []
        for f in range(4):
            src = box.at[:, f * 256 : (f + 1) * 256]
            slot = 2 * z_low + core
            send, recv = ms_send.at[index + f], ms_recv.at[index + 4 + slot]
            here = stay & (z == f)

            @pl.when(here)
            def _():
                pltpu.make_async_copy(src, got_rows(got, slot), recv).start()

            @pl.when(jnp.logical_not(here))
            def _():
                remote(src, got_rows(got, slot), send, recv, (2 * place.chip + z_high, f))

            copies.append((src, send, here))

        def wait():
            for src, send, here in copies:

                @pl.when(jnp.logical_not(here))
                def _():
                    pltpu.make_async_remote_copy(
                        src_ref=src, dst_ref=got_rows(got, 0), send_sem=send, recv_sem=ms_recv.at[index + 4],
                        device_id=place.at(core=1), device_id_type=MESH,
                    ).wait_send()

            for slot in range(4):
                pltpu.make_async_copy(
                    box.at[:, 0:256], got_rows(got, slot), ms_recv.at[index + 4 + slot]
                ).wait()

        return wait

    def output_rows(start):
        rows = pl.ds(start, 32)
        value = res[rows, :] + acc_out[own_rows(32, start), :] + got_out[rows, :].astype(F32)
        box[rows, :] = (value + vec[7:8, :]).astype(BF)

    def join_rows(got, dst):
        split, shared = SEQ - CORE_ROWS, FULL - CORE_ROWS
        last = 2 * SEQ
        even, odd = CORE_ROWS, 3 * CORE_ROWS
        dst[0:CORE_ROWS, :] = got[0:CORE_ROWS, :].astype(F32)
        dst[CORE_ROWS:SEQ, :] = got[even : even + split, :].astype(F32)
        dst[SEQ : SEQ + HALF, :] = got[even + shared : even + shared + HALF, :].astype(F32)
        dst[SEQ + HALF : last, :] = got[odd + shared : odd + shared + HALF, :].astype(F32)[1:, :]
        dst[last : last + CORE_ROWS, :] = got[2 * CORE_ROWS : odd, :].astype(F32)
        dst[last + CORE_ROWS :, :] = got[odd : odd + split, :].astype(F32)

    tiles(CORE_ROWS, 32, output_rows)
    wait_out = send_out(out_got, 16)
    for pair in range(4):
        attend_back(pair)
        if pair == 2:
            weight_grad(OUT, ln_two, OWN, mixed)
        if pair < 3:
            scatter_to(6 + pair)
    weight_grad(4, ln_one, ALL, v)
    scatter_to(9)
    weight_grad(5, ln_one, ALL, k)
    wait_out()
    join_rows(out_got, input_grad)
    output[...] = input_grad[...].astype(BF)

    def one_part(rows, size):
        value = dot(k[rows, :], w[KEY], (1, 1)) + dot(v[rows, :], w[VALUE], (1, 1))
        return value + dot(q[rows, :], w[QUERY], (1, 1))

    def one_other(start):
        box[pl.ds(start, 224), :] = one_part(other_rows(224, start), 224).astype(BF)

    tiles(CORE_ROWS, 224, one_other)
    copy_one = swap(box, got_half, 11, place.at(core=1))
    scatter_to(10)
    weight_grad(6, ln_one, OWN, q)

    value = dot(k[OWN:, :], w[KEY], (1, 1)) + dot(v[OWN:, :], w[VALUE], (1, 1))
    acc_out[0:PART, :] = value
    rest = got_pair.at[0]
    rest_rows = slice(0, PART)
    rest[...] = acc_out[rest_rows, :].astype(BF)

    def rest_copy():
        return pltpu.make_async_remote_copy(
            src_ref=rest, dst_ref=got_rest, send_sem=ms_send.at[12], recv_sem=ms_recv.at[12],
            device_id=place.at(core=1), device_id_type=MESH,
        )

    @pl.when(core == 0)
    def _():
        rest_copy().start()

    def one_own(start):
        rows = own_rows(224, start)
        res[pl.ds(start, 224), :] = one_part(rows, 224)

    tiles(CORE_ROWS, 224, one_own)

    def pair_copy():
        return pltpu.make_async_remote_copy(
            src_ref=rest, dst_ref=got_pair.at[1], send_sem=ms_send.at[13], recv_sem=ms_recv.at[13],
            device_id=place.at(z=1), device_id_type=MESH,
        )

    @pl.when(core == 0)
    def _():
        rest_copy().wait_send()

    @pl.when(core == 1)
    def _():
        rest_copy().wait_recv()
        rest[...] = (acc_out[rest_rows, :] + got_rest[...].astype(F32)).astype(BF)
        pair_copy().start()

    scatter_to(11)

    def sum_heads(ref, size):
        def body(start):
            value = ref[pl.ds(start, 16), :].astype(F32)
            pre[0:8, :] += row_sum(value)

        pre[0:8, :] = jnp.zeros((8, pre.shape[1]), F32)
        tiles(size, 16, body)
        return jnp.sum(pre[0:8, :], axis=0, keepdims=True)

    def spread(value):
        left = jnp.where(core == 0, value, 0.0)
        right = jnp.where(core == 0, 0.0, value)
        size = place.columns
        parts = []
        for i in range(place.zs):
            parts += [left[:, i * size : (i + 1) * size], right[:, i * size : (i + 1) * size]]
        return jnp.concatenate(parts, axis=1)

    vec_sum[...] = jnp.zeros_like(vec_sum)
    vec_sum[4:5, :] = spread(sum_heads(q, OWN))
    vec_sum[5:6, :] = spread(sum_heads(v, ALL))
    copy_one.wait()

    @pl.when(core == 1)
    def _():
        pair_copy().wait()
        start = FULL - CORE_ROWS
        res[start:, :] = res[start:, :] + got_pair[1].astype(F32)

    def back_one(start):
        rows, held = pl.ds(start, 16), own_rows(16, start)
        normed, inv_std = normalize(x[held, :].astype(F32))
        grad = res[rows, :] + got_half[rows, :].astype(F32)
        sums[0] += row_sum(grad * normed)
        sums[1] += row_sum(grad)
        value = acc_two[held, :] + normalize_back(grad * vec[0:1, :], normed, inv_std)
        box[rows, :] = value.astype(BF)

    tiles(CORE_ROWS, 16, back_one)
    wait_grad = send_out(grad_got, 24)
    for row in (0, 1, 2, 3, 6, 7):
        vec_sum[row : row + 1, :] = jnp.sum(sums[row], axis=0, keepdims=True)
    ups = [jnp.sum(up_sums[piece], axis=0, keepdims=True) for piece in range(PIECES)]
    for i in range(place.zs):
        size = place.columns
        row = jnp.concatenate([up[:, i * size : (i + 1) * size] for up in ups], axis=1)
        left, right = jnp.where(core == 0, row, 0.0), jnp.where(core == 0, 0.0, row)
        vec_sum[8 + i : 9 + i, :] = jnp.concatenate((left, right), axis=1)

    vec_steps = sum_steps(place, vec_sum, vec_slots, vs_send, vs_recv)
    next(vec_steps, None)
    for tick in range(12, scatter_last + 1):
        scatter_to(tick)
        next(vec_steps, None)
    for _ in vec_steps:
        pass
    norm_sum[...] = jnp.zeros_like(norm_sum)

    @pl.loop(0, ITEMS)
    def _(i):
        value = fin[i].astype(F32)
        norm_sum[...] += jnp.sum((value * value).reshape(-1, 8, value.shape[-1]), axis=0)

    norm_steps = sum_steps(place, norm_sum, norm_slots, ns_send, ns_recv)
    next(norm_steps)
    wait_grad()
    join_rows(grad_got, input_grad)
    for i in range(ITEMS):
        for h in range(2):
            value = fin[i, h].astype(F32)
            if i < 4:
                attn_grad[:, i, h * place.columns : (h + 1) * place.columns] = value
            else:
                at = (h * PIECES + (i - 4) // 2) * place.columns
                mlp_grad[:, i % 2, at : at + place.columns] = value
    for _ in norm_steps:
        pass
    rows = lax.broadcasted_iota(jnp.int32, vec_sum.shape, 0)
    held = jnp.where(rows < vec.shape[0], vec_sum[...], 0.0)
    total = jnp.sum(norm_sum[...], keepdims=True) + jnp.sum(held * held, keepdims=True)
    norm_out[...] = jnp.broadcast_to(jnp.sqrt(total), norm_out.shape)


def run_layer(attn_weights, mlp_weights, inputs, cotangent, vec):
    width = vec.shape[1]
    rows, columns = attn_weights.shape[0], attn_weights.shape[2] // 2
    token_count, features = inputs.shape
    chips = lax.axis_size("dp") // 2
    bits = chips.bit_length() - 1
    heads = 4 * columns
    hops = bits + 3
    block = 2 * rows
    whole = pl.BlockSpec(memory_space=pltpu.VMEM)

    def buf(*shape, dtype=BF):
        return pltpu.VMEM(shape, dtype)

    gather_copies = 5 + 2 * chips + bits
    scatter_copies = 2 * (chips - 1) + 4
    scratch = [
        buf(ITEMS, width, heads),
        buf(ITEMS, rows, columns),
        buf(ITEMS, 2, rows, columns),
        buf(4 * CORE_ROWS, features),
        buf(4 * CORE_ROWS, features),
        buf(8, 128, dtype=F32),
        buf(ALL, width),
        buf(ALL, width),
        buf(ALL, heads),
        buf(ALL, heads),
        buf(ALL, heads),
        buf(OWN, heads),
        buf(OWN, heads, dtype=F32),
        buf(OWN, width),
        buf(OWN, width),
        buf(OWN, width, dtype=F32),
        buf(OWN, width, dtype=F32),
        buf(CORE_ROWS, width, dtype=F32),
        buf(CORE_ROWS, heads, dtype=F32),
        buf(CORE_ROWS, heads, dtype=F32),
        buf(OWN, heads),
        buf(OWN, heads),
        buf(CORE_ROWS, width),
        buf(CORE_ROWS, width),
        buf(CORE_ROWS, width),
        buf(PART, width),
        buf(2, PART, width),
        buf(SLOTS, (chips - 1) * block, heads),
        buf(SLOTS, block, 3 * columns),
        buf(8, 8, width, dtype=F32),
        buf(PIECES, 8, heads, dtype=F32),
        buf(2 * hops, 16, width, dtype=F32),
        buf(2 * hops, 8, 128, dtype=F32),
        pltpu.SemaphoreType.DMA((ITEMS, gather_copies)),
        pltpu.SemaphoreType.DMA((ITEMS, gather_copies)),
        pltpu.SemaphoreType.DMA((ITEMS, scatter_copies)),
        pltpu.SemaphoreType.DMA((ITEMS, scatter_copies)),
        pltpu.SemaphoreType.DMA((9, 3)),
        pltpu.SemaphoreType.DMA((9, 3)),
        pltpu.SemaphoreType.DMA((32,)),
        pltpu.SemaphoreType.DMA((32,)),
        pltpu.SemaphoreType.DMA((hops,)),
        pltpu.SemaphoreType.DMA((hops,)),
        pltpu.SemaphoreType.DMA((hops,)),
        pltpu.SemaphoreType.DMA((hops,)),
    ]
    return pl.pallas_call(
        layer_kernel,
        in_specs=[whole] * 5,
        out_specs=[whole] * 6,
        out_shape=[
            jax.ShapeDtypeStruct((token_count, features), BF),
            jax.ShapeDtypeStruct((token_count, features), F32),
            jax.ShapeDtypeStruct(attn_weights.shape, F32),
            jax.ShapeDtypeStruct(mlp_weights.shape, F32),
            jax.ShapeDtypeStruct((16, width), F32),
            jax.ShapeDtypeStruct((8, 128), F32),
        ],
        scratch_shapes=scratch,
        compiler_params=pltpu.CompilerParams(
            collective_id=0, has_side_effects=True, vmem_limit_bytes=VMEM_LIMIT
        ),
        name="layer",
    )(attn_weights, mlp_weights, inputs, cotangent, vec)


def adam_step(weight, grad, mean, square, rate, decay):
    next_mean = beta_one * mean + (1.0 - beta_one) * grad
    next_square = beta_two * square + (1.0 - beta_two) * grad * grad
    mean_hat = next_mean / (1.0 - beta_one**STEP)
    square_hat = next_square / (1.0 - beta_two**STEP)
    updated = weight - rate * (mean_hat / (jnp.sqrt(square_hat) + adam_eps) + decay * weight)
    return (updated, next_mean, next_square)


def shards(
    inputs,
    cotangent,
    attn_weights,
    mlp_weights,
    vectors,
    attn_mean,
    mlp_mean,
    vector_mean,
    attn_square,
    mlp_square,
    vector_square,
):
    tensor_count = lax.axis_size("tensor")
    data_count = lax.axis_size("dp")
    token_count, feature_local = inputs.shape
    width = feature_local * tensor_count
    hidden_cols = mlp_weights.shape[2]
    assert tensor_count == 4 and token_count == 3 * SEQ
    assert attn_weights.shape[2] * PIECES == hidden_cols == width

    output, input_grad, attn_grad, mlp_grad, vec_sum, norm_out = run_layer(
        attn_weights, mlp_weights, inputs, cotangent, vectors
    )
    vector_grad = vec_sum[: vectors.shape[0]]
    grad_norm = norm_out[0, 0]
    clip_limit = clip_ratio * math.sqrt(width * hidden_cols * tensor_count * token_count * data_count)
    factor = jnp.minimum(1.0, clip_limit / (grad_norm + norm_eps))
    updated_attn, next_attn_mean, next_attn_square = adam_step(
        attn_weights, factor * attn_grad, attn_mean, attn_square, rate_matrix, decay_matrix
    )
    updated_mlp, next_mlp_mean, next_mlp_square = adam_step(
        mlp_weights, factor * mlp_grad, mlp_mean, mlp_square, rate_matrix, decay_matrix
    )
    updated_vectors, next_vector_mean, next_vector_square = adam_step(
        vectors, factor * vector_grad, vector_mean, vector_square, rate_vector, 0.0
    )
    return (
        output,
        input_grad,
        grad_norm,
        updated_attn,
        updated_mlp,
        updated_vectors,
        next_attn_mean,
        next_mlp_mean,
        next_vector_mean,
        next_attn_square,
        next_mlp_square,
        next_vector_square,
    )


def solution(mesh):
    rows = P("dp", "tensor")
    weight = P("dp", None, "tensor")
    return jax.shard_map(
        shards,
        mesh=mesh,
        in_specs=(rows, rows) + (weight, weight, P()) * 3,
        out_specs=(rows, rows, P()) + (weight, weight, P()) * 3,
        check_vma=False,
    )
```

```python
import math

import jax
import jax.numpy as jnp
from jax import lax
from jax.experimental import pallas as pl
from jax.experimental.pallas import tpu as pltpu
from jax.sharding import PartitionSpec as P

HD = 64
SEQ = 577
STEP = 10

beta_one = 0.9
beta_two = 0.999
rate_matrix = 0.1
rate_vector = 0.5
decay_matrix = 0.1
adam_eps = 1e-08
norm_eps = 1e-06
clip_ratio = 0.025

BF = jnp.bfloat16
F32 = jnp.float32

FULL = 592
PART = 304
HALF = SEQ // 2 + 1
OWN = FULL + PART
ALL = OWN + PART
CORE_ROWS = OWN // 2
PIECES = 4
ITEMS = 4 + 2 * PIECES
VMEM_LIMIT = 64 * 2**20
SLOTS = 6
COLUMN_SLOTS = 8
GATHER_SLOTS = 8
QUERY, KEY, VALUE, OUT = range(4)
MESH = pl.DeviceIdType.MESH


def dot(left, right, dims):
    return lax.dot_general(left, right, ((dims[:1], dims[1:]), ((), ())), preferred_element_type=F32)


def xor(index, mask):
    out = index
    bit = 1
    while bit <= mask:
        if mask & bit:
            out = out + bit * (1 - 2 * ((index // bit) % 2))
        bit *= 2
    return out


def normalize(rows_in):
    center = rows_in - jnp.mean(rows_in, axis=-1, keepdims=True)
    inv_std = lax.rsqrt(jnp.mean(center * center, axis=-1, keepdims=True) + norm_eps)
    return center * inv_std, inv_std


def normalize_back(scaled, normed, inv_std):
    return inv_std * (
        scaled
        - jnp.mean(scaled, axis=-1, keepdims=True)
        - normed * jnp.mean(scaled * normed, axis=-1, keepdims=True)
    )


def gelu_parts(u):
    a = jnp.abs(u)
    t = 1.0 / (1.0 + (0.3275911 / math.sqrt(2.0)) * a)
    e = jnp.exp(-0.5 * u * u)
    poly = t * (
        0.254829592 + t * (-0.284496736 + t * (1.421413741 + t * (-1.453152027 + t * 1.061405429)))
    )
    tail = 0.5 * poly * e
    phi_big = jnp.where(u >= 0, 1.0 - tail, tail)
    return phi_big, u * e * (1.0 / math.sqrt(2.0 * math.pi))


class Place:
    def __init__(self, rows, columns):
        self.dp = lax.axis_index("dp")
        self.z = lax.axis_index("tensor")
        self.core = self.dp % 2
        self.chip = self.dp // 2
        self.chips = lax.axis_size("dp") // 2
        self.zs = lax.axis_size("tensor")
        self.core_rows = rows
        self.rows = 2 * rows
        self.columns = columns
        count = self.chips.bit_length() - 1
        fast = [1 << i for i in range((count + 1) // 2)]
        slow = [1 << i for i in range((count + 1) // 2, count)]
        self.orders = (fast + slow, slow + fast)
        self.z_bits = [1 << i for i in range(self.zs.bit_length() - 1)]

    def at(self, core=0, chip=0, z=0):
        return (xor(self.dp, core + 2 * chip), xor(self.z, z))

    def chip_rows(self, mask, count=1):
        return pl.ds(pl.multiple_of(xor(self.chip, mask) * self.rows, self.rows), count * self.rows)

    def z_columns(self, mask):
        return pl.ds(pl.multiple_of(xor(self.z, mask) * self.columns, self.columns), self.columns)

    def half_rows(self, core):
        start = self.chip * self.rows + core * self.core_rows
        return pl.ds(pl.multiple_of(start, self.core_rows), self.core_rows)


def remote(src, dst, send, recv, device):
    copy = pltpu.make_async_remote_copy(
        src_ref=src, dst_ref=dst, send_sem=send, recv_sem=recv, device_id=device, device_id_type=MESH
    )
    copy.start()
    return copy


def gather_steps(place, weight, send_sem, recv_sem):
    used = [0]

    def send(rows, columns, device):
        ref = weight.at[rows, columns]
        k = used[0]
        used[0] += 1
        return remote(ref, ref, send_sem.at[k], recv_sem.at[k], device)

    have = [0]
    for bit in reversed(place.z_bits):
        copies = [send(place.chip_rows(0), place.z_columns(m), place.at(z=bit)) for m in have]
        yield
        for copy in copies:
            copy.wait()
        have = have + [m ^ bit for m in have]
    width = place.zs * place.columns
    parts = (slice(0, width // 2), slice(width // 2, width))
    haves = [[0], [0]]
    for step in range(len(place.orders[0])):
        copies = []
        for i, columns in enumerate(parts):
            bit = place.orders[i][step]
            masks = sorted(haves[i])
            count = len(masks)
            if masks == list(range(count)):
                start = place.chip // count * count
                rows = pl.ds(pl.multiple_of(start * place.rows, place.rows), count * place.rows)
                copies.append(send(rows, columns, place.at(chip=bit)))
            else:
                for m in masks:
                    copies.append(send(place.chip_rows(m), columns, place.at(chip=bit)))
            haves[i] = masks + [m ^ bit for m in masks]
        yield
        for copy in copies:
            copy.wait()


def add_block(ref, rows, columns, other):
    ref[rows, columns] = (ref[rows, columns].astype(F32) + other.astype(F32)).astype(BF)


def scatter_steps(place, weight, by_rows, by_columns, final, send_sem, recv_sem):
    used = [0]

    def send(src, dst, device):
        k = used[0]
        used[0] += 1
        return remote(src, dst, send_sem.at[k], recv_sem.at[k], device)

    width = place.zs * place.columns
    parts = (slice(0, width // 2), slice(width // 2, width))
    haves = [list(range(place.chips))] * 2
    base = 0
    for step in reversed(range(len(place.orders[0]))):
        copies, adds = [], []
        bits = [order[step] for order in place.orders]
        haves = [[m for m in have if not m & bit] for have, bit in zip(haves, bits)]
        for slot in range(len(haves[0])):
            there = pl.ds(base + slot * place.rows, place.rows)
            for columns, bit, have in zip(parts, bits, haves):
                m = have[slot]
                src = weight.at[place.chip_rows(m ^ bit), columns]
                copies.append(send(src, by_rows.at[there, columns], place.at(chip=bit)))
                adds.append((place.chip_rows(m), columns, there))
        base += len(haves[0]) * place.rows
        yield
        for copy in copies:
            copy.wait()
        for rows, columns, there in adds:
            add_block(weight, rows, columns, by_rows[there, columns])
    have = list(range(place.zs))
    base = 0
    for bit in place.z_bits:
        keep = [m for m in have if not m & bit]
        copies, adds = [], []
        for slot, m in enumerate(keep):
            there = pl.ds(base + slot * place.columns, place.columns)
            src = weight.at[place.chip_rows(0), place.z_columns(m ^ bit)]
            copies.append(send(src, by_columns.at[:, there], place.at(z=bit)))
            adds.append((m, there))
        base += len(keep) * place.columns
        have = keep
        yield
        for copy in copies:
            copy.wait()
        for m, there in adds:
            add_block(weight, place.chip_rows(0), place.z_columns(m), by_columns[:, there])
    other = weight.at[place.half_rows(1 - place.core), place.z_columns(0)]
    copy = send(other, final.at[place.core], place.at(core=1))
    final[pl.ds(place.core, 1)] = weight[place.half_rows(place.core), place.z_columns(0)][None]
    yield
    copy.wait()


def sum_steps(place, value, result, parts, send_sem, recv_sem):
    size = value.shape[1] // 8
    here = place.core * place.zs + place.z
    used = [0]

    def columns(index):
        return pl.ds(pl.multiple_of(index * size, size), size)

    def send(src, dst, partner):
        k = used[0]
        used[0] += 1
        return remote(src, dst, send_sem.at[k], recv_sem.at[k], partner)

    others = [(k // 4, k % 4) for k in range(1, 8)]
    parts[pl.ds(here, 1)] = value[:, columns(here)][None]
    copies = []
    for c, m in others:
        there = xor(place.core, c) * place.zs + xor(place.z, m)
        copies.append(send(value.at[:, columns(there)], parts.at[here], place.at(core=c, z=m)))
    yield
    for copy in copies:
        copy.wait()
    total = parts[0]
    for k in range(1, 8):
        total = total + parts[k]
    parts[pl.ds(8 + place.chip, 1)] = total[None]
    mine = parts.at[8 + place.chip]
    copies = [send(mine, mine, place.at(chip=k)) for k in range(1, place.chips)]
    yield
    for copy in copies:
        copy.wait()
    total = parts[8]
    for k in range(1, place.chips):
        total = total + parts[8 + k]
    result[:, columns(here)] = total
    mine = result.at[:, columns(here)]
    copies = [send(mine, mine, place.at(core=c, z=m)) for c, m in others]
    yield
    for copy in copies:
        copy.wait()


def sum_quickly(place, value, slots, send_sem, recv_sem):
    others = [place.at(core=k // 4, z=k % 4) for k in range(1, 8)]
    column = (place.core * place.zs + place.z, 8, 0, others)
    chips = (place.chip, place.chips, 8, [place.at(chip=k) for k in range(1, place.chips)])
    for here, count, base, partners in (column, chips):
        slots[pl.ds(base + here, 1)] = value[...][None]
        slot = slots.at[base + here]
        copies = [
            remote(slot, slot, send_sem.at[base + k], recv_sem.at[base + k], partner)
            for k, partner in enumerate(partners)
        ]
        yield
        for copy in copies:
            copy.wait()
        total = slots[base]
        for k in range(1, count):
            total = total + slots[base + k]
        value[...] = total


def layer_kernel(
    attn_in, mlp_hbm, inputs_hbm, cot_hbm, vec,
    output, input_grad, attn_grad, mlp_grad, vec_sum, norm_out,
    w, theirs, inputs, cotangent, fin, out_got, grad_got, norm_sum, x, ln_one, q, k, v, mixed, lse, cot, ln_two, acc_out, acc_two, res, pre, gh, hid, gp,
    box, got_half, got_out, got_rest, got_pair, by_rows, by_columns,
    sums, up_sums, vec_part, vec_slots, norm_slots,
    ag_send, ag_recv, rs_send, rs_recv, xs_send, xs_recv, ms_send, ms_recv, vs_send, vs_recv, ns_send, ns_recv,
):
    width = x.shape[1]
    place = Place(fin.shape[2], fin.shape[3])
    core, z = place.core, place.z
    z_low = z % 2
    z_high = z // 2


    mlp_in = mlp_grad
    barrier = pltpu.get_barrier_semaphore()
    for c in range(2):
        for m in range(4):
            if c or m:
                pl.semaphore_signal(barrier, inc=1, device_id=place.at(core=c, z=m), device_id_type=MESH)
    for chip in range(1, place.chips):
        pl.semaphore_signal(barrier, inc=1, device_id=place.at(chip=chip), device_id_type=MESH)
    loads = [
        pltpu.make_async_copy(src, dst, ms_send.at[24 + i])
        for i, (src, dst) in enumerate(((mlp_hbm, mlp_in), (inputs_hbm, inputs), (cot_hbm, cotangent)))
    ]
    for load in loads:
        load.start()

    gathers = [
        gather_steps(place, w.at[i], ag_send.at[i % GATHER_SLOTS], ag_recv.at[i % GATHER_SLOTS])
        for i in range(ITEMS)
    ]
    steps = len(place.orders[0])
    offsets = [0, 1] + [2 + 2 * s for s in range(steps + 1)]
    entry_tick = [max(i // 2, i - 2) for i in range(ITEMS)]
    gather_events = sorted(
        (entry_tick[i] + offset, -s, i) for i in range(ITEMS) for s, offset in enumerate(offsets)
    )
    gather_last = gather_events[-1][0]

    def gather_item(item):
        gather_to(entry_tick[item] + offsets[-1])

    tick = {"gather": 0}

    def gather_to(now):
        while gather_events and gather_events[0][0] <= now:
            next(gathers[gather_events.pop(0)[2]], None)
        tick["gather"] = max(tick["gather"], now)

    scatter_order = [(i, i) for i in range(4, ITEMS)]
    scatter_order += [(OUT, OUT), (VALUE, 4), (KEY, 5), (QUERY, 6)]
    scatters = [
        scatter_steps(
            place, w.at[slot], by_rows.at[n % SLOTS], by_columns.at[n % COLUMN_SLOTS], fin.at[i],
            rs_send.at[n % COLUMN_SLOTS], rs_recv.at[n % COLUMN_SLOTS],
        )
        for n, (i, slot) in enumerate(scatter_order)
    ]
    stage = [0] * ITEMS

    def advance(*which):
        for n in which:
            for _ in range(steps - 1 if stage[n] == 2 else 1):
                next(scatters[n], None)
            stage[n] += 1

    def pump():
        if tick["gather"] < gather_last:
            gather_to(tick["gather"] + 1)

    def swap(src, dst, index, device):
        return remote(src, dst, ms_send.at[index], ms_recv.at[index], device)

    stay = core == z_high

    SECTIONS = []
    odd_full = FULL + 2 * PART
    for start, size, even, odd in (
        (0, FULL, 0, odd_full), (FULL, PART, FULL, OWN), (OWN, PART, OWN, FULL)
    ):
        cuts = (208, 192, 192) if size == FULL else (160, 144)
        for cut in cuts:
            SECTIONS.append((start, cut, even, odd))
            start, even, odd = start + cut, even + cut, odd + cut

    def send_rows(src, dst, section, chunk):
        start, size, even, odd = SECTIONS[section]
        columns = pl.ds(pl.multiple_of(z * src.shape[1], src.shape[1]), src.shape[1])
        rows = pl.ds(start, size)
        there = dst.at[rows, columns]
        first = pl.multiple_of(even + z_low * (odd - even), 16)
        second = pl.multiple_of(odd + z_low * (even - odd), 16)
        src_same, src_cross = src.at[pl.ds(first, size), :], src.at[pl.ds(second, size), :]
        target = (2 * place.chip + z_high, 2 * core + z_low)
        other = (2 * place.chip + z_high, 2 * core + 1 - z_low)

        @pl.when(stay)
        def _():
            pltpu.make_async_copy(src_same, there, xs_recv.at[chunk, 0]).start()

        @pl.when(jnp.logical_not(stay))
        def _():
            remote(src_same, there, xs_send.at[chunk, 0], xs_recv.at[chunk, 0], target)

        copy = remote(src_cross, there, xs_send.at[chunk, 1], xs_recv.at[chunk, 1], other)

        def wait():
            whole = pltpu.make_async_remote_copy(
                src_ref=src_same, dst_ref=there, send_sem=xs_send.at[chunk, 0],
                recv_sem=xs_recv.at[chunk, 0], device_id=other, device_id_type=MESH,
            )

            @pl.when(jnp.logical_not(stay))
            def _():
                whole.wait_send()

            whole.wait_recv()
            copy.wait()

            half = width // 2
            here = dst.at[rows, pl.ds(pl.multiple_of(core * half, half), half)]
            return remote(here, here, xs_send.at[chunk, 2], xs_recv.at[chunk, 2], place.at(core=1))

        return wait

    def own_rows(size, start=0):
        return pl.ds(pl.multiple_of(core * CORE_ROWS + start, 16), size)

    def other_rows(size, start=0):
        return pl.ds(pl.multiple_of((1 - core) * CORE_ROWS + start, 16), size)

    def tiles(total, size, body):
        @pl.loop(0, total // size)
        def _(t):
            body(pl.multiple_of(t * size, size))

    def norm_rows(start):
        rows = pl.ds(start, 80)
        normed, _ = normalize(x[rows, :].astype(F32))
        ln_one[rows, :] = (normed * vec[0:1, :] + vec[1:2, :]).astype(BF)

    def head_bias(row):
        size = place.columns
        parts = []
        for i in range(place.zs):
            low = vec[row : row + 1, 2 * i * size : (2 * i + 1) * size]
            high = vec[row : row + 1, (2 * i + 1) * size : (2 * i + 2) * size]
            parts.append(jnp.where(core == 0, low, high))
        return jnp.concatenate(parts, axis=1)

    def up_bias(piece):
        size = place.columns
        parts = []
        for i in range(place.zs):
            low = vec[8 + i : 9 + i, piece * size : (piece + 1) * size]
            high = vec[8 + i : 9 + i, (PIECES + piece) * size : (PIECES + piece + 1) * size]
            parts.append(jnp.where(core == 0, low, high))
        return jnp.concatenate(parts, axis=1)

    def project(item, dst, bias):
        def body(start):
            rows = pl.ds(start, 240)
            value = dot(ln_one[rows, :], w[item], (1, 0))
            if bias is not None:
                value = value + bias
            dst[rows, :] = value.astype(BF)

        tiles(ALL, 240, body)

    IMAGES = ((0, FULL, FULL), (FULL, PART, 2 * PART))

    def masked(q_in, k_in, low):
        scores = dot(q_in, k_in, (1, 1)) * HD**-0.5
        col = lax.broadcasted_iota(jnp.int32, scores.shape, 1)
        if low:
            inside = jnp.where(col < PART, col, col - PART)
            good = (inside < HALF) & (col != PART * (1 - z_low))
        else:
            good = col < SEQ
        return jnp.where(good, scores, -1e30)

    def attend(pair):
        lanes = pl.ds(pl.multiple_of(pair * 2 * HD, 2 * HD), 2 * HD)
        for low, size, keys in IMAGES:
            q_in, k_in, v_in = q[low : low + size, lanes], k[low : low + keys, lanes], v[low : low + keys, lanes]
            outs, logs = [], []
            for head in range(2):
                cut = slice(head * HD, (head + 1) * HD)
                scores = masked(q_in[:, cut], k_in[:, cut], low)
                peaks = jnp.max(scores, axis=-1, keepdims=True)
                exponent = jnp.exp(scores - peaks)
                totals = jnp.sum(exponent, axis=-1, keepdims=True)
                probs = (exponent * (1.0 / totals)).astype(BF)
                outs.append(dot(probs, v_in[:, cut], (1, 0)))
                logs.append(jnp.broadcast_to(peaks + jnp.log(totals), (size, HD)))
            mixed[low : low + size, lanes] = jnp.concatenate(outs, axis=1).astype(BF)
            lse[low : low + size, lanes] = jnp.concatenate(logs, axis=1)

    def attend_back(pair):
        lanes = pl.ds(pl.multiple_of(pair * 2 * HD, 2 * HD), 2 * HD)
        scale = HD**-0.5
        for low, size, keys in IMAGES:
            q_in, k_in, v_in = q[low : low + size, lanes], k[low : low + keys, lanes], v[low : low + keys, lanes]
            do_in, o_in = hid[low : low + size, lanes], mixed[low : low + size, lanes]
            logs = lse[low : low + size, lanes]
            dqs, dks, dvs = [], [], []
            for head in range(2):
                cut = slice(head * HD, (head + 1) * HD)
                do = do_in[:, cut]
                scores = masked(q_in[:, cut], k_in[:, cut], low)
                probs = jnp.exp(scores - logs[:, head * HD : head * HD + 1])
                grad_probs = dot(do, v_in[:, cut], (1, 1))
                delta = jnp.sum(do.astype(F32) * o_in[:, cut].astype(F32), axis=-1, keepdims=True)
                ds = (probs * (grad_probs - delta)).astype(BF)
                dqs.append(dot(ds, k_in[:, cut], (1, 0)) * scale)
                dks.append(dot(ds, q_in[:, cut], (0, 0)) * scale)
                dvs.append(dot(probs.astype(BF), do, (0, 0)))
            q[low : low + size, lanes] = jnp.concatenate(dqs, axis=1).astype(BF)
            k[low : low + keys, lanes] = jnp.concatenate(dks, axis=1).astype(BF)
            v[low : low + keys, lanes] = jnp.concatenate(dvs, axis=1).astype(BF)

    def row_sum(value):
        return jnp.sum(value.reshape(-1, 8, value.shape[-1]), axis=0)

    def split_weights(i):
        if i < 4:
            low, high = (attn_in[:, i, h * place.columns : (h + 1) * place.columns] for h in range(2))
        else:
            piece, which = (i - 4) // 2, i % 2
            at = [(h * PIECES + piece) * place.columns for h in range(2)]
            low, high = (mlp_in[:, which, t : t + place.columns] for t in at)
        low, high = low.astype(BF), high.astype(BF)
        w[i, place.half_rows(core), place.z_columns(0)] = jnp.where(core == 0, low, high)
        theirs[i] = jnp.where(core == 0, high, low)

    def swap_weights(first, count, index):
        there = w.at[pl.ds(first, count), place.half_rows(core), place.z_columns(0)]
        return swap(theirs.at[pl.ds(first, count)], there, index, place.at(core=1))

    def split_rows(src, dst):
        middle, last = SEQ + HALF, 2 * SEQ
        whole = input_grad
        whole[...] = src[...].astype(F32)
        gap = jnp.zeros((FULL - SEQ, src.shape[1]), F32)
        dst[0:FULL, :] = jnp.concatenate((whole[0:SEQ, :], gap)).astype(BF)
        dst[FULL:OWN, :] = jnp.concatenate((whole[SEQ:middle, :], gap)).astype(BF)
        upper = jnp.concatenate((gap[0:1], whole[middle:last, :], gap))
        dst[OWN:ALL, :] = upper.astype(BF)
        dst[ALL:, :] = jnp.concatenate((whole[last:, :], gap)).astype(BF)

    for i in range(4):
        split_weights(i)
    pl.semaphore_wait(barrier, 7 + place.chips - 1)
    copy_weights = swap_weights(0, 4, 0)
    loads[0].wait()
    copy_weights.wait()
    gather_to(0)
    for i in range(4, ITEMS):
        split_weights(i)
    copy_weights = swap_weights(4, ITEMS - 4, 1)
    loads[1].wait()
    split_rows(inputs, out_got)
    copy_weights.wait()
    gather_to(2)
    waits, swaps, done = [], [], 0

    def send_cot(chunk):
        cot_waits.append(send_rows(grad_got, cot, chunk, 7 + chunk))

    parts = ((0, 1), (2, 3), (4, 5), (6,))
    for n, part in enumerate(parts):
        for chunk in part:
            waits.append(send_rows(out_got, x, chunk, chunk))
        pump()
        for chunk in part:
            swaps.append(waits[chunk]())
        if n == 1:
            loads[2].wait()
            split_rows(cotangent, grad_got)
        if n:
            for chunk in parts[n - 1]:
                swaps[chunk].wait()
            while done + 80 <= SECTIONS[chunk][0] + SECTIONS[chunk][1]:
                norm_rows(done)
                done += 80
    cot_waits, cot_swaps = [], []
    send_cot(0)
    swaps[6].wait()

    def norm_more(start):
        norm_rows(pl.multiple_of(done + start, 16))

    tiles(ALL - done, 80, norm_more)
    pump()
    gather_item(KEY)
    project(QUERY, q, head_bias(4))
    project(KEY, k, None)
    pump()
    send_cot(1)
    gather_item(VALUE)
    project(VALUE, v, head_bias(5))
    for pair in range(4):
        attend(pair)
        if pair % 2:
            pump()
        if pair < 3:
            cot_swaps.append(cot_waits[pair]())
            send_cot(2 + pair)

    gather_item(OUT)
    def out_other(start):
        rows = other_rows(224, start)
        box[pl.ds(start, 224), :] = dot(mixed[rows, :], w[OUT], (1, 1)).astype(BF)

    tiles(CORE_ROWS, 224, out_other)
    copy_attn = swap(box, got_half, 6, place.at(core=1))

    def out_own(start):
        rows = own_rows(224, start)
        value = dot(mixed[rows, :], w[OUT], (1, 1))
        res[pl.ds(start, 224), :] = value + x[rows, :].astype(F32) + vec[6:7, :]

    tiles(CORE_ROWS, 224, out_own)
    copy_attn.wait()

    def norm_two(start):
        rows = pl.ds(start, 32)
        value = res[rows, :] + got_half[rows, :].astype(F32)
        res[rows, :] = value
        normed, _ = normalize(value)
        ln_two[own_rows(32, start), :] = (normed * vec[2:3, :] + vec[3:4, :]).astype(BF)

    tiles(CORE_ROWS, 32, norm_two)
    mine_two = ln_two.at[own_rows(CORE_ROWS), :]
    copy_two = swap(mine_two, mine_two, 7, place.at(core=1))
    pump()
    cot_swaps.append(cot_waits[3]())
    cot_swaps.append(cot_waits[4]())
    gather_item(5)
    for copy in cot_swaps:
        copy.wait()
    copy_two.wait()

    up_sums[...] = jnp.zeros_like(up_sums)

    def mlp_piece(piece, hook):
        up, down = 4 + 2 * piece, 5 + 2 * piece
        gather_item(down)
        bias = up_bias(piece)

        def rows_part(start):
            rows = pl.ds(start, CORE_ROWS)
            pre[...] = dot(ln_two[rows, :], w[up], (1, 0))
            gh[...] = dot(cot[rows, :], w[down], (1, 0))

            def activate(at):
                inside = pl.ds(at, 32)
                u = pre[inside, :] + bias
                cdf, slope = gelu_parts(u)
                grad = (gh[inside, :] * (cdf + slope)).astype(BF)
                hid[pl.ds(start + at, 32), :] = (u * cdf).astype(BF)
                gp[pl.ds(start + at, 32), :] = grad
                up_sums[piece] += row_sum(grad.astype(F32))

            tiles(CORE_ROWS, 32, activate)
            out = dot(hid[rows, :], w[down], (1, 1))
            two = dot(gp[rows, :], w[up], (1, 1))
            if piece:
                acc_out[rows, :] += out
                acc_two[rows, :] += two
            else:
                acc_out[rows, :] = out
                acc_two[rows, :] = two

        tiles(OWN, CORE_ROWS, rows_part)
        hook()

        def up_rows(start):
            rows = pl.ds(start, 256)
            w[up, rows, :] = dot(ln_two[:, rows], gp[...], (0, 0)).astype(BF)
            w[down, rows, :] = dot(cot[:, rows], hid[...], (0, 0)).astype(BF)

        tiles(width, 256, up_rows)

    def nothing():
        pass

    def gather_near(left):
        return lambda: gather_to(gather_last - left)

    mlp_piece(0, gather_near(4))
    gather_near(3)()
    advance(0)
    mlp_piece(1, gather_near(2))
    advance(1)
    mlp_piece(2, lambda: None)
    gather_near(1)()
    advance(2, 0)
    mlp_piece(3, lambda: None)
    advance(3, 1, 0)

    def send_half(acc, start):
        box[pl.ds(start, 64), :] = acc[other_rows(64, start), :].astype(BF)

    tiles(CORE_ROWS, 64, lambda start: send_half(acc_two, start))
    copy_two = swap(box, got_half, 8, place.at(core=1))
    sums[...] = jnp.zeros_like(sums)
    copy_two.wait()

    def back_two(start):
        rows, held = pl.ds(start, 32), own_rows(32, start)
        normed, inv_std = normalize(res[rows, :])
        grad = acc_two[held, :] + got_half[rows, :].astype(F32)
        grad_out = cot[held, :].astype(F32)
        acc_two[held, :] = grad_out + normalize_back(grad * vec[2:3, :], normed, inv_std)
        sums[2] += row_sum(grad * normed)
        sums[3] += row_sum(grad)
        sums[6] += row_sum(acc_two[held, :])
        sums[7] += row_sum(grad_out)
        ln_two[held, :] = acc_two[held, :].astype(BF)

    tiles(CORE_ROWS, 32, back_two)
    advance(4, 0)
    mine_two = ln_two.at[own_rows(CORE_ROWS), :]
    copy_grad = swap(mine_two, mine_two, 9, place.at(core=1))
    tiles(CORE_ROWS, 64, lambda start: send_half(acc_out, start))
    copy_out = swap(box, got_out, 10, place.at(core=1))
    copy_grad.wait()

    def grad_heads(start):
        rows = pl.ds(start, CORE_ROWS)
        hid[rows, :] = dot(ln_two[rows, :], w[OUT], (1, 0)).astype(BF)

    tiles(OWN, CORE_ROWS, grad_heads)
    advance(5, 2, 1, 0)

    def weight_grad(item, left, size, right):
        def body(start):
            rows = pl.ds(start, 256)
            w[item, rows, :] = dot(left[0:size, rows], right[0:size, :], (0, 0)).astype(BF)

        tiles(width, 256, body)

    pump()

    def got_rows(got, slot):
        return got.at[pl.ds(pl.multiple_of(slot * CORE_ROWS, CORE_ROWS), CORE_ROWS), :]

    class SendRows:
        def __init__(self, got, index):
            self.got, self.index = got, index
            self.slot = 2 * z_low + core

        def start(self, first, size):
            rows = pl.ds(first, size)
            there = pl.ds(pl.multiple_of(self.slot * CORE_ROWS + first, 16), size)
            for f in range(4):
                src, dst = box.at[rows, f * 256 : (f + 1) * 256], self.got.at[there, :]
                recv = ms_recv.at[self.index + 4 + self.slot]
                here = stay & (z == f)

                @pl.when(here)
                def _():
                    pltpu.make_async_copy(src, dst, recv).start()

                @pl.when(jnp.logical_not(here))
                def _():
                    remote(src, dst, ms_send.at[self.index + f], recv, (2 * place.chip + z_high, f))

        def wait(self):
            for f in range(4):
                src = box.at[:, f * 256 : (f + 1) * 256]

                @pl.when(jnp.logical_not(stay & (z == f)))
                def _():
                    pltpu.make_async_remote_copy(
                        src_ref=src, dst_ref=got_rows(self.got, 0), send_sem=ms_send.at[self.index + f],
                        recv_sem=ms_recv.at[self.index + 4], device_id=place.at(core=1), device_id_type=MESH,
                    ).wait_send()

            for slot in range(4):
                recv = ms_recv.at[self.index + 4 + slot]
                pltpu.make_async_copy(box.at[:, 0:256], got_rows(self.got, slot), recv).wait()

    def output_rows(start):
        rows = pl.ds(start, 32)
        value = res[rows, :] + acc_out[own_rows(32, start), :] + got_out[rows, :].astype(F32)
        box[rows, :] = (value + vec[7:8, :]).astype(BF)

    def join_rows(got, dst):
        split, shared = SEQ - CORE_ROWS, FULL - CORE_ROWS
        last = 2 * SEQ
        even, odd = CORE_ROWS, 3 * CORE_ROWS
        dst[0:CORE_ROWS, :] = got[0:CORE_ROWS, :].astype(F32)
        dst[CORE_ROWS:SEQ, :] = got[even : even + split, :].astype(F32)
        dst[SEQ : SEQ + HALF, :] = got[even + shared : even + shared + HALF, :].astype(F32)
        dst[SEQ + HALF : last, :] = got[odd + shared : odd + shared + HALF, :].astype(F32)[1:, :]
        dst[last : last + CORE_ROWS, :] = got[2 * CORE_ROWS : odd, :].astype(F32)
        dst[last + CORE_ROWS :, :] = got[odd : odd + split, :].astype(F32)

    copy_out.wait()
    tiles(CORE_ROWS, 32, output_rows)
    send_output = SendRows(out_got, 16)
    send_output.start(0, 112)
    weight_grad(OUT, ln_two, OWN, mixed)
    for pair in range(4):
        attend_back(pair)
        advance(*((3, 1, 0), (6, 2, 1), (7, 4, 3, 2), (8, 5, 1))[pair])
        if pair < 3:
            send_output.start(112 * (pair + 1), 112)
    def one_part(rows, size):
        value = dot(k[rows, :], w[KEY], (1, 1)) + dot(v[rows, :], w[VALUE], (1, 1))
        return value + dot(q[rows, :], w[QUERY], (1, 1))

    rest = got_pair.at[0]
    rest_rows = slice(0, PART)

    def rest_copy():
        return pltpu.make_async_remote_copy(
            src_ref=rest, dst_ref=got_rest, send_sem=ms_send.at[12], recv_sem=ms_recv.at[12],
            device_id=place.at(core=1), device_id_type=MESH,
        )

    def pair_copy():
        return pltpu.make_async_remote_copy(
            src_ref=rest, dst_ref=got_pair.at[1], send_sem=ms_send.at[13], recv_sem=ms_recv.at[13],
            device_id=place.at(z=1), device_id_type=MESH,
        )

    def one_other(start):
        cot[pl.ds(start, 224), :] = one_part(other_rows(224, start), 224).astype(BF)

    tiles(CORE_ROWS, 224, one_other)
    copy_one = swap(cot.at[0:CORE_ROWS, :], got_half, 11, place.at(core=1))
    value = dot(k[OWN:, :], w[KEY], (1, 1)) + dot(v[OWN:, :], w[VALUE], (1, 1))
    acc_out[0:PART, :] = value
    rest[...] = acc_out[rest_rows, :].astype(BF)

    @pl.when(core == 0)
    def _():
        rest_copy().start()

    weight_grad(4, ln_one, ALL, v)
    advance(4, 6, 9)

    @pl.when(core == 0)
    def _():
        rest_copy().wait_send()

    @pl.when(core == 1)
    def _():
        rest_copy().wait_recv()
        rest[...] = (acc_out[rest_rows, :] + got_rest[...].astype(F32)).astype(BF)
        pair_copy().start()

    weight_grad(5, ln_one, ALL, k)
    advance(3, 2)

    def one_own(start):
        rows = own_rows(224, start)
        res[pl.ds(start, 224), :] = one_part(rows, 224)

    tiles(CORE_ROWS, 224, one_own)
    send_output.wait()
    copy_one.wait()

    @pl.when(core == 1)
    def _():
        pair_copy().wait()
        start = FULL - CORE_ROWS
        res[start:, :] = res[start:, :] + got_pair[1].astype(F32)

    def back_one(start):
        rows, held = pl.ds(start, 32), own_rows(32, start)
        normed, inv_std = normalize(x[held, :].astype(F32))
        grad = res[rows, :] + got_half[rows, :].astype(F32)
        sums[0] += row_sum(grad * normed)
        sums[1] += row_sum(grad)
        value = acc_two[held, :] + normalize_back(grad * vec[0:1, :], normed, inv_std)
        box[rows, :] = value.astype(BF)

    tiles(CORE_ROWS, 32, back_one)
    send_grad = SendRows(grad_got, 24)
    send_grad.start(0, 112)
    advance(2, 5, 7, 10)
    assert stage[:3] == [6] * 3
    weight_grad(6, ln_one, OWN, q)
    send_grad.start(112, 112)
    advance(6, 8, 11)

    def sum_heads(ref, size):
        def body(start):
            value = ref[pl.ds(start, 16), :].astype(F32)
            pre[0:8, :] += row_sum(value)

        pre[0:8, :] = jnp.zeros((8, pre.shape[1]), F32)
        tiles(size, 16, body)
        return jnp.sum(pre[0:8, :], axis=0, keepdims=True)

    def spread(value):
        left = jnp.where(core == 0, value, 0.0)
        right = jnp.where(core == 0, 0.0, value)
        size = place.columns
        parts = []
        for i in range(place.zs):
            parts += [left[:, i * size : (i + 1) * size], right[:, i * size : (i + 1) * size]]
        return jnp.concatenate(parts, axis=1)

    vec_part[...] = jnp.zeros_like(vec_part)
    ups = [jnp.sum(up_sums[piece], axis=0, keepdims=True) for piece in range(PIECES)]
    for i in range(place.zs):
        size = place.columns
        row = jnp.concatenate([up[:, i * size : (i + 1) * size] for up in ups], axis=1)
        left, right = jnp.where(core == 0, row, 0.0), jnp.where(core == 0, 0.0, row)
        vec_part[8 + i : 9 + i, :] = jnp.concatenate((left, right), axis=1)
    vec_part[4:5, :] = spread(sum_heads(q, OWN))
    vec_part[5:6, :] = spread(sum_heads(v, ALL))
    for row in (0, 1, 2, 3, 6, 7):
        vec_part[row : row + 1, :] = jnp.sum(sums[row], axis=0, keepdims=True)
    vec_steps = sum_steps(place, vec_part, vec_sum, vec_slots, vs_send, vs_recv)
    next(vec_steps)
    join_rows(out_got, input_grad)
    output[...] = input_grad[...].astype(BF)
    advance(7, 9, 3, 4, 5)
    send_grad.start(224, 112)
    advance(6, 8, 10, 3, 4, 5, 7)
    send_grad.start(336, 112)
    advance(6, 9, 11, 4, 8, 5, 7, 6, 10, 9, 8, 11, 7)
    next(vec_steps)
    advance(10, 9, 8, 11)
    next(vec_steps)
    advance(10, 9, 11, 10, 11)
    assert stage == [6] * ITEMS
    for _ in vec_steps:
        pass
    norm_sum[...] = jnp.zeros_like(norm_sum)

    @pl.loop(0, ITEMS)
    def _(i):
        value = fin[i].astype(F32)
        norm_sum[...] += jnp.sum((value * value).reshape(-1, 8, value.shape[-1]), axis=0)

    norm_steps = sum_quickly(place, norm_sum, norm_slots, ns_send, ns_recv)
    next(norm_steps)
    send_grad.wait()
    join_rows(grad_got, input_grad)
    for i in range(ITEMS):
        for h in range(2):
            value = fin[i, h].astype(F32)
            if i < 4:
                attn_grad[:, i, h * place.columns : (h + 1) * place.columns] = value
            else:
                at = (h * PIECES + (i - 4) // 2) * place.columns
                mlp_grad[:, i % 2, at : at + place.columns] = value
    for _ in norm_steps:
        pass
    rows = lax.broadcasted_iota(jnp.int32, vec_sum.shape, 0)
    held = jnp.where(rows < vec.shape[0], vec_sum[...], 0.0)
    total = jnp.sum(norm_sum[...], keepdims=True) + jnp.sum(held * held, keepdims=True)
    norm_out[...] = jnp.broadcast_to(jnp.sqrt(total), norm_out.shape)


def run_layer(attn_weights, mlp_weights, inputs, cotangent, vec):
    width = vec.shape[1]
    rows, columns = attn_weights.shape[0], attn_weights.shape[2] // 2
    token_count, features = inputs.shape
    chips = lax.axis_size("dp") // 2
    bits = chips.bit_length() - 1
    heads = 4 * columns
    slots = 8 + chips
    block = 2 * rows
    whole = pl.BlockSpec(memory_space=pltpu.VMEM)
    hbm = pl.BlockSpec(memory_space=pl.ANY)

    def buf(*shape, dtype=BF):
        return pltpu.VMEM(shape, dtype)

    gather_copies = 3 + bits + chips - 1
    scatter_copies = 2 * (chips - 1) + 4
    scratch = [
        buf(ITEMS, width, heads),
        buf(ITEMS, rows, columns),
        buf(token_count, features),
        buf(token_count, features),
        buf(ITEMS, 2, rows, columns),
        buf(4 * CORE_ROWS, features),
        buf(4 * CORE_ROWS, features),
        buf(8, 128, dtype=F32),
        buf(ALL, width),
        buf(ALL, width),
        buf(ALL, heads),
        buf(ALL, heads),
        buf(ALL, heads),
        buf(OWN, heads),
        buf(OWN, heads, dtype=F32),
        buf(OWN, width),
        buf(OWN, width),
        buf(OWN, width, dtype=F32),
        buf(OWN, width, dtype=F32),
        buf(CORE_ROWS, width, dtype=F32),
        buf(CORE_ROWS, heads, dtype=F32),
        buf(CORE_ROWS, heads, dtype=F32),
        buf(OWN, heads),
        buf(OWN, heads),
        buf(CORE_ROWS, width),
        buf(CORE_ROWS, width),
        buf(CORE_ROWS, width),
        buf(PART, width),
        buf(2, PART, width),
        buf(SLOTS, (chips - 1) * block, heads),
        buf(COLUMN_SLOTS, block, 3 * columns),
        buf(8, 8, width, dtype=F32),
        buf(PIECES, 8, heads, dtype=F32),
        buf(16, width, dtype=F32),
        buf(8 + chips, 16, width // 8, dtype=F32),
        buf(slots, 8, 128, dtype=F32),
        pltpu.SemaphoreType.DMA((GATHER_SLOTS, gather_copies)),
        pltpu.SemaphoreType.DMA((GATHER_SLOTS, gather_copies)),
        pltpu.SemaphoreType.DMA((COLUMN_SLOTS, scatter_copies)),
        pltpu.SemaphoreType.DMA((COLUMN_SLOTS, scatter_copies)),
        pltpu.SemaphoreType.DMA((12, 3)),
        pltpu.SemaphoreType.DMA((12, 3)),
        pltpu.SemaphoreType.DMA((32,)),
        pltpu.SemaphoreType.DMA((32,)),
        pltpu.SemaphoreType.DMA((14 + chips,)),
        pltpu.SemaphoreType.DMA((14 + chips,)),
        pltpu.SemaphoreType.DMA((slots,)),
        pltpu.SemaphoreType.DMA((slots,)),
    ]
    return pl.pallas_call(
        layer_kernel,
        in_specs=[whole, hbm, hbm, hbm, whole],
        out_specs=[whole] * 6,
        out_shape=[
            jax.ShapeDtypeStruct((token_count, features), BF),
            jax.ShapeDtypeStruct((token_count, features), F32),
            jax.ShapeDtypeStruct(attn_weights.shape, F32),
            jax.ShapeDtypeStruct(mlp_weights.shape, F32),
            jax.ShapeDtypeStruct((16, width), F32),
            jax.ShapeDtypeStruct((8, 128), F32),
        ],
        scratch_shapes=scratch,
        compiler_params=pltpu.CompilerParams(
            collective_id=0, has_side_effects=True, vmem_limit_bytes=VMEM_LIMIT
        ),
        name="layer",
    )(attn_weights, mlp_weights, inputs, cotangent, vec)


def adam_step(weight, grad, mean, square, rate, decay):
    next_mean = beta_one * mean + (1.0 - beta_one) * grad
    next_square = beta_two * square + (1.0 - beta_two) * grad * grad
    mean_hat = next_mean / (1.0 - beta_one**STEP)
    square_hat = next_square / (1.0 - beta_two**STEP)
    updated = weight - rate * (mean_hat / (jnp.sqrt(square_hat) + adam_eps) + decay * weight)
    return (updated, next_mean, next_square)


def shards(
    inputs,
    cotangent,
    attn_weights,
    mlp_weights,
    vectors,
    attn_mean,
    mlp_mean,
    vector_mean,
    attn_square,
    mlp_square,
    vector_square,
):
    tensor_count = lax.axis_size("tensor")
    data_count = lax.axis_size("dp")
    token_count, feature_local = inputs.shape
    width = feature_local * tensor_count
    hidden_cols = mlp_weights.shape[2]
    assert tensor_count == 4 and token_count == 3 * SEQ
    assert attn_weights.shape[2] * PIECES == hidden_cols == width

    output, input_grad, attn_grad, mlp_grad, vec_sum, norm_out = run_layer(
        attn_weights, mlp_weights, inputs, cotangent, vectors
    )
    vector_grad = vec_sum[: vectors.shape[0]]
    grad_norm = norm_out[0, 0]
    clip_limit = clip_ratio * math.sqrt(width * hidden_cols * tensor_count * token_count * data_count)
    factor = jnp.minimum(1.0, clip_limit / (grad_norm + norm_eps))

    def adam_flat(*arrays):
        rows, groups, columns = arrays[0].shape
        weight, grad, mean, square = (
            a.reshape(rows, groups, columns // 128, 128).swapaxes(1, 2).reshape(-1, 128) for a in arrays
        )
        results = adam_step(weight, factor * grad, mean, square, rate_matrix, decay_matrix)
        return tuple(
            a.reshape(rows, columns // 128, groups, 128).swapaxes(1, 2).reshape(rows, groups, columns)
            for a in results
        )

    updated_attn, next_attn_mean, next_attn_square = adam_flat(
        attn_weights, attn_grad, attn_mean, attn_square
    )
    updated_mlp, next_mlp_mean, next_mlp_square = adam_flat(mlp_weights, mlp_grad, mlp_mean, mlp_square)
    updated_vectors, next_vector_mean, next_vector_square = adam_step(
        vectors, factor * vector_grad, vector_mean, vector_square, rate_vector, 0.0
    )
    return (
        output,
        input_grad,
        grad_norm,
        updated_attn,
        updated_mlp,
        updated_vectors,
        next_attn_mean,
        next_mlp_mean,
        next_vector_mean,
        next_attn_square,
        next_mlp_square,
        next_vector_square,
    )


def solution(mesh):
    rows = P("dp", "tensor")
    weight = P("dp", None, "tensor")
    return jax.shard_map(
        shards,
        mesh=mesh,
        in_specs=(rows, rows) + (weight, weight, P()) * 3,
        out_specs=(rows, rows, P()) + (weight, weight, P()) * 3,
        check_vma=False,
    )
```

```python
import functools
import math

import jax
import jax.numpy as jnp
from jax import lax
from jax.experimental import pallas as pl
from jax.experimental.pallas import tpu as pltpu
from jax.sharding import PartitionSpec as P

HD = 64
SEQ = 577
STEP = 10

beta_one = 0.9
beta_two = 0.999
rate_matrix = 0.1
rate_vector = 0.5
decay_matrix = 0.1
adam_eps = 1e-08
norm_eps = 1e-06
clip_ratio = 0.025

BF = jnp.bfloat16
F32 = jnp.float32

FULL = 592
PART = 304
HALF = SEQ // 2 + 1
OWN = FULL + PART
ALL = OWN + PART
CORE_ROWS = OWN // 2
PIECES = 4
ITEMS = 4 + 2 * PIECES
VMEM_LIMIT = 64 * 2**20
SLOTS = 6
COLUMN_SLOTS = 8
GATHER_SLOTS = 8
QUERY, KEY, VALUE, OUT = range(4)
MESH = pl.DeviceIdType.MESH


def dot(left, right, dims):
    return lax.dot_general(left, right, ((dims[:1], dims[1:]), ((), ())), preferred_element_type=F32)


def xor(index, mask):
    out = index
    bit = 1
    while bit <= mask:
        if mask & bit:
            out = out + bit * (1 - 2 * ((index // bit) % 2))
        bit *= 2
    return out


def normalize(rows_in):
    center = rows_in - jnp.mean(rows_in, axis=-1, keepdims=True)
    inv_std = lax.rsqrt(jnp.mean(center * center, axis=-1, keepdims=True) + norm_eps)
    return center * inv_std, inv_std


def normalize_back(scaled, normed, inv_std):
    return inv_std * (
        scaled
        - jnp.mean(scaled, axis=-1, keepdims=True)
        - normed * jnp.mean(scaled * normed, axis=-1, keepdims=True)
    )


def gelu_parts(u):
    a = jnp.abs(u)
    t = 1.0 / (1.0 + (0.3275911 / math.sqrt(2.0)) * a)
    e = jnp.exp(-0.5 * u * u)
    poly = t * (
        0.254829592 + t * (-0.284496736 + t * (1.421413741 + t * (-1.453152027 + t * 1.061405429)))
    )
    tail = 0.5 * poly * e
    phi_big = jnp.where(u >= 0, 1.0 - tail, tail)
    return phi_big, u * e * (1.0 / math.sqrt(2.0 * math.pi))


class Place:
    def __init__(self, rows, columns):
        self.dp = lax.axis_index("dp")
        self.z = lax.axis_index("tensor")
        self.core = self.dp % 2
        self.chip = self.dp // 2
        self.chips = lax.axis_size("dp") // 2
        self.zs = lax.axis_size("tensor")
        self.core_rows = rows
        self.rows = 2 * rows
        self.columns = columns
        count = self.chips.bit_length() - 1
        fast = [1 << i for i in range((count + 1) // 2)]
        slow = [1 << i for i in range((count + 1) // 2, count)]
        self.orders = (fast + slow, slow + fast)
        self.z_bits = [1 << i for i in range(self.zs.bit_length() - 1)]

    def at(self, core=0, chip=0, z=0):
        return (xor(self.dp, core + 2 * chip), xor(self.z, z))

    def chip_rows(self, mask, count=1):
        return pl.ds(pl.multiple_of(xor(self.chip, mask) * self.rows, self.rows), count * self.rows)

    def z_columns(self, mask):
        return pl.ds(pl.multiple_of(xor(self.z, mask) * self.columns, self.columns), self.columns)

    def half_rows(self, core):
        start = self.chip * self.rows + core * self.core_rows
        return pl.ds(pl.multiple_of(start, self.core_rows), self.core_rows)


def remote(src, dst, send, recv, device):
    copy = pltpu.make_async_remote_copy(
        src_ref=src, dst_ref=dst, send_sem=send, recv_sem=recv, device_id=device, device_id_type=MESH
    )
    copy.start()
    return copy


def gather_steps(place, weight, send_sem, recv_sem):
    used = [0]

    def send(rows, columns, device):
        ref = weight.at[rows, columns]
        k = used[0]
        used[0] += 1
        return remote(ref, ref, send_sem.at[k], recv_sem.at[k], device)

    have = [0]
    for bit in reversed(place.z_bits):
        copies = [send(place.chip_rows(0), place.z_columns(m), place.at(z=bit)) for m in have]
        yield
        for copy in copies:
            copy.wait()
        have = have + [m ^ bit for m in have]
    width = place.zs * place.columns
    parts = (slice(0, width // 2), slice(width // 2, width))
    haves = [[0], [0]]
    for step in range(len(place.orders[0])):
        copies = []
        for i, columns in enumerate(parts):
            bit = place.orders[i][step]
            masks = sorted(haves[i])
            count = len(masks)
            if masks == list(range(count)):
                start = place.chip // count * count
                rows = pl.ds(pl.multiple_of(start * place.rows, place.rows), count * place.rows)
                copies.append(send(rows, columns, place.at(chip=bit)))
            else:
                for m in masks:
                    copies.append(send(place.chip_rows(m), columns, place.at(chip=bit)))
            haves[i] = masks + [m ^ bit for m in masks]
        yield
        for copy in copies:
            copy.wait()


def add_block(ref, rows, columns, other):
    ref[rows, columns] = (ref[rows, columns].astype(F32) + other.astype(F32)).astype(BF)


def scatter_steps(place, weight, by_rows, by_columns, final, send_sem, recv_sem):
    used = [0]

    def send(src, dst, device):
        k = used[0]
        used[0] += 1
        return remote(src, dst, send_sem.at[k], recv_sem.at[k], device)

    width = place.zs * place.columns
    parts = (slice(0, width // 2), slice(width // 2, width))
    haves = [list(range(place.chips))] * 2
    base = 0
    for step in reversed(range(len(place.orders[0]))):
        copies, adds = [], []
        bits = [order[step] for order in place.orders]
        haves = [[m for m in have if not m & bit] for have, bit in zip(haves, bits)]
        for slot in range(len(haves[0])):
            there = pl.ds(base + slot * place.rows, place.rows)
            for columns, bit, have in zip(parts, bits, haves):
                m = have[slot]
                src = weight.at[place.chip_rows(m ^ bit), columns]
                copies.append(send(src, by_rows.at[there, columns], place.at(chip=bit)))
                adds.append((place.chip_rows(m), columns, there))
        base += len(haves[0]) * place.rows
        yield
        for copy in copies:
            copy.wait()
        for rows, columns, there in adds:
            add_block(weight, rows, columns, by_rows[there, columns])
    have = list(range(place.zs))
    base = 0
    for bit in place.z_bits:
        keep = [m for m in have if not m & bit]
        copies, adds = [], []
        for slot, m in enumerate(keep):
            there = pl.ds(base + slot * place.columns, place.columns)
            src = weight.at[place.chip_rows(0), place.z_columns(m ^ bit)]
            copies.append(send(src, by_columns.at[:, there], place.at(z=bit)))
            adds.append((m, there))
        base += len(keep) * place.columns
        have = keep
        yield
        for copy in copies:
            copy.wait()
        for m, there in adds:
            add_block(weight, place.chip_rows(0), place.z_columns(m), by_columns[:, there])
    other = weight.at[place.half_rows(1 - place.core), place.z_columns(0)]
    copy = send(other, final.at[place.core], place.at(core=1))
    final[pl.ds(place.core, 1)] = weight[place.half_rows(place.core), place.z_columns(0)][None]
    yield
    copy.wait()


def sum_steps(place, value, result, parts, send_sem, recv_sem):
    size = value.shape[1] // 8
    here = place.core * place.zs + place.z
    used = [0]

    def columns(index):
        return pl.ds(pl.multiple_of(index * size, size), size)

    def send(src, dst, partner):
        k = used[0]
        used[0] += 1
        return remote(src, dst, send_sem.at[k], recv_sem.at[k], partner)

    others = [(k // 4, k % 4) for k in range(1, 8)]
    parts[pl.ds(here, 1)] = value[:, columns(here)][None]
    copies = []
    for c, m in others:
        there = xor(place.core, c) * place.zs + xor(place.z, m)
        copies.append(send(value.at[:, columns(there)], parts.at[here], place.at(core=c, z=m)))
    yield
    for copy in copies:
        copy.wait()
    total = parts[0]
    for k in range(1, 8):
        total = total + parts[k]
    parts[pl.ds(8 + place.chip, 1)] = total[None]
    mine = parts.at[8 + place.chip]
    copies = [send(mine, mine, place.at(chip=k)) for k in range(1, place.chips)]
    yield
    for copy in copies:
        copy.wait()
    total = parts[8]
    for k in range(1, place.chips):
        total = total + parts[8 + k]
    result[:, columns(here)] = total
    mine = result.at[:, columns(here)]
    copies = [send(mine, mine, place.at(core=c, z=m)) for c, m in others]
    yield
    for copy in copies:
        copy.wait()


def sum_quickly(place, value, slots, send_sem, recv_sem):
    others = [place.at(core=k // 4, z=k % 4) for k in range(1, 8)]
    column = (place.core * place.zs + place.z, 8, 0, others)
    chips = (place.chip, place.chips, 8, [place.at(chip=k) for k in range(1, place.chips)])
    for here, count, base, partners in (column, chips):
        slots[pl.ds(base + here, 1)] = value[...][None]
        slot = slots.at[base + here]
        copies = [
            remote(slot, slot, send_sem.at[base + k], recv_sem.at[base + k], partner)
            for k, partner in enumerate(partners)
        ]
        yield
        for copy in copies:
            copy.wait()
        total = slots[base]
        for k in range(1, count):
            total = total + slots[base + k]
        value[...] = total


def layer_kernel(
    attn_in, mlp_hbm, inputs_hbm, cot_hbm, vec,
    output, input_grad, attn_grad, mlp_grad, vec_sum, norm_out,
    w, theirs, inputs, cotangent, fin, out_got, grad_got, norm_sum, x, ln_one, q, k, v, mixed, lse, cot, ln_two, acc_out, acc_two, res, pre, gh, hid, gp,
    box, got_half, got_out, got_rest, got_pair, by_rows, by_columns,
    sums, up_sums, vec_part, vec_slots, norm_slots,
    ag_send, ag_recv, rs_send, rs_recv, xs_send, xs_recv, ms_send, ms_recv, vs_send, vs_recv, ns_send, ns_recv,
):
    width = x.shape[1]
    place = Place(fin.shape[2], fin.shape[3])
    core, z = place.core, place.z
    z_low = z % 2
    z_high = z // 2


    mlp_in = mlp_grad
    barrier = pltpu.get_barrier_semaphore()
    for c in range(2):
        for m in range(4):
            if c or m:
                pl.semaphore_signal(barrier, inc=1, device_id=place.at(core=c, z=m), device_id_type=MESH)
    for chip in range(1, place.chips):
        pl.semaphore_signal(barrier, inc=1, device_id=place.at(chip=chip), device_id_type=MESH)
    loads = [
        pltpu.make_async_copy(src, dst, ms_send.at[24 + i])
        for i, (src, dst) in enumerate(((mlp_hbm, mlp_in), (inputs_hbm, inputs), (cot_hbm, cotangent)))
    ]
    for load in loads:
        load.start()

    gathers = [
        gather_steps(place, w.at[i], ag_send.at[i % GATHER_SLOTS], ag_recv.at[i % GATHER_SLOTS])
        for i in range(ITEMS)
    ]
    steps = len(place.orders[0])
    offsets = [0, 1] + [2 + 2 * s for s in range(steps + 1)]
    entry_tick = [max(i // 2, i - 2) for i in range(ITEMS)]
    gather_events = sorted(
        (entry_tick[i] + offset, -s, i) for i in range(ITEMS) for s, offset in enumerate(offsets)
    )
    gather_last = gather_events[-1][0]

    def gather_item(item):
        gather_to(entry_tick[item] + offsets[-1])

    tick = {"gather": 0}

    def gather_to(now):
        while gather_events and gather_events[0][0] <= now:
            next(gathers[gather_events.pop(0)[2]], None)
        tick["gather"] = max(tick["gather"], now)

    scatter_order = [(i, i) for i in range(4, ITEMS)]
    scatter_order += [(OUT, OUT), (VALUE, 4), (KEY, 5), (QUERY, 6)]
    scatters = [
        scatter_steps(
            place, w.at[slot], by_rows.at[n % SLOTS], by_columns.at[n % COLUMN_SLOTS], fin.at[i],
            rs_send.at[n % COLUMN_SLOTS], rs_recv.at[n % COLUMN_SLOTS],
        )
        for n, (i, slot) in enumerate(scatter_order)
    ]
    stage = [0] * ITEMS

    def advance(*which):
        for n in which:
            for _ in range(steps - 1 if stage[n] == 2 else 1):
                next(scatters[n], None)
            stage[n] += 1

    def pump():
        if tick["gather"] < gather_last:
            gather_to(tick["gather"] + 1)

    def swap(src, dst, index, device):
        return remote(src, dst, ms_send.at[index], ms_recv.at[index], device)

    stay = core == z_high

    SECTIONS = []
    odd_full = FULL + 2 * PART
    for start, size, even, odd in (
        (0, FULL, 0, odd_full), (FULL, PART, FULL, OWN), (OWN, PART, OWN, FULL)
    ):
        cuts = (208, 192, 192) if size == FULL else (160, 144)
        for cut in cuts:
            SECTIONS.append((start, cut, even, odd))
            start, even, odd = start + cut, even + cut, odd + cut

    def send_rows(src, dst, section, chunk):
        start, size, even, odd = SECTIONS[section]
        columns = pl.ds(pl.multiple_of(z * src.shape[1], src.shape[1]), src.shape[1])
        rows = pl.ds(start, size)
        there = dst.at[rows, columns]
        first = pl.multiple_of(even + z_low * (odd - even), 16)
        second = pl.multiple_of(odd + z_low * (even - odd), 16)
        src_same, src_cross = src.at[pl.ds(first, size), :], src.at[pl.ds(second, size), :]
        target = (2 * place.chip + z_high, 2 * core + z_low)
        other = (2 * place.chip + z_high, 2 * core + 1 - z_low)

        @pl.when(stay)
        def _():
            pltpu.make_async_copy(src_same, there, xs_recv.at[chunk, 0]).start()

        @pl.when(jnp.logical_not(stay))
        def _():
            remote(src_same, there, xs_send.at[chunk, 0], xs_recv.at[chunk, 0], target)

        copy = remote(src_cross, there, xs_send.at[chunk, 1], xs_recv.at[chunk, 1], other)

        def wait():
            whole = pltpu.make_async_remote_copy(
                src_ref=src_same, dst_ref=there, send_sem=xs_send.at[chunk, 0],
                recv_sem=xs_recv.at[chunk, 0], device_id=other, device_id_type=MESH,
            )

            @pl.when(jnp.logical_not(stay))
            def _():
                whole.wait_send()

            whole.wait_recv()
            copy.wait()

            half = width // 2
            here = dst.at[rows, pl.ds(pl.multiple_of(core * half, half), half)]
            return remote(here, here, xs_send.at[chunk, 2], xs_recv.at[chunk, 2], place.at(core=1))

        return wait

    def own_rows(size, start=0):
        return pl.ds(pl.multiple_of(core * CORE_ROWS + start, 16), size)

    def other_rows(size, start=0):
        return pl.ds(pl.multiple_of((1 - core) * CORE_ROWS + start, 16), size)

    def tiles(total, size, body):
        @pl.loop(0, total // size)
        def _(t):
            body(pl.multiple_of(t * size, size))

    def norm_rows(start):
        rows = pl.ds(start, 80)
        normed, _ = normalize(x[rows, :].astype(F32))
        ln_one[rows, :] = (normed * vec[0:1, :] + vec[1:2, :]).astype(BF)

    def head_bias(row):
        size = place.columns
        parts = []
        for i in range(place.zs):
            low = vec[row : row + 1, 2 * i * size : (2 * i + 1) * size]
            high = vec[row : row + 1, (2 * i + 1) * size : (2 * i + 2) * size]
            parts.append(jnp.where(core == 0, low, high))
        return jnp.concatenate(parts, axis=1)

    def up_bias(piece):
        size = place.columns
        parts = []
        for i in range(place.zs):
            low = vec[8 + i : 9 + i, piece * size : (piece + 1) * size]
            high = vec[8 + i : 9 + i, (PIECES + piece) * size : (PIECES + piece + 1) * size]
            parts.append(jnp.where(core == 0, low, high))
        return jnp.concatenate(parts, axis=1)

    def project(item, dst, bias):
        def body(start):
            rows = pl.ds(start, 240)
            value = dot(ln_one[rows, :], w[item], (1, 0))
            if bias is not None:
                value = value + bias
            dst[rows, :] = value.astype(BF)

        tiles(ALL, 240, body)

    IMAGES = ((0, FULL, FULL), (FULL, PART, 2 * PART))

    def masked(q_in, k_in, low):
        scores = dot(q_in, k_in, (1, 1)) * HD**-0.5
        col = lax.broadcasted_iota(jnp.int32, scores.shape, 1)
        if low:
            inside = jnp.where(col < PART, col, col - PART)
            good = (inside < HALF) & (col != PART * (1 - z_low))
        else:
            good = col < SEQ
        return jnp.where(good, scores, -1e30)

    def attend(pair):
        lanes = pl.ds(pl.multiple_of(pair * 2 * HD, 2 * HD), 2 * HD)
        for low, size, keys in IMAGES:
            q_in, k_in, v_in = q[low : low + size, lanes], k[low : low + keys, lanes], v[low : low + keys, lanes]
            outs, logs = [], []
            for head in range(2):
                cut = slice(head * HD, (head + 1) * HD)
                scores = masked(q_in[:, cut], k_in[:, cut], low)
                peaks = jnp.max(scores, axis=-1, keepdims=True)
                exponent = jnp.exp(scores - peaks)
                totals = jnp.sum(exponent, axis=-1, keepdims=True)
                probs = (exponent * (1.0 / totals)).astype(BF)
                outs.append(dot(probs, v_in[:, cut], (1, 0)))
                logs.append(jnp.broadcast_to(peaks + jnp.log(totals), (size, HD)))
            mixed[low : low + size, lanes] = jnp.concatenate(outs, axis=1).astype(BF)
            lse[low : low + size, lanes] = jnp.concatenate(logs, axis=1)

    def attend_back(pair):
        lanes = pl.ds(pl.multiple_of(pair * 2 * HD, 2 * HD), 2 * HD)
        scale = HD**-0.5
        for low, size, keys in IMAGES:
            q_in, k_in, v_in = q[low : low + size, lanes], k[low : low + keys, lanes], v[low : low + keys, lanes]
            do_in, o_in = hid[low : low + size, lanes], mixed[low : low + size, lanes]
            logs = lse[low : low + size, lanes]
            dqs, dks, dvs = [], [], []
            for head in range(2):
                cut = slice(head * HD, (head + 1) * HD)
                do = do_in[:, cut]
                scores = masked(q_in[:, cut], k_in[:, cut], low)
                probs = jnp.exp(scores - logs[:, head * HD : head * HD + 1])
                grad_probs = dot(do, v_in[:, cut], (1, 1))
                delta = jnp.sum(do.astype(F32) * o_in[:, cut].astype(F32), axis=-1, keepdims=True)
                ds = (probs * (grad_probs - delta)).astype(BF)
                dqs.append(dot(ds, k_in[:, cut], (1, 0)) * scale)
                dks.append(dot(ds, q_in[:, cut], (0, 0)) * scale)
                dvs.append(dot(probs.astype(BF), do, (0, 0)))
            q[low : low + size, lanes] = jnp.concatenate(dqs, axis=1).astype(BF)
            k[low : low + keys, lanes] = jnp.concatenate(dks, axis=1).astype(BF)
            v[low : low + keys, lanes] = jnp.concatenate(dvs, axis=1).astype(BF)

    def row_sum(value):
        return jnp.sum(value.reshape(-1, 8, value.shape[-1]), axis=0)

    def split_weights(i):
        if i < 4:
            low, high = (attn_in[:, i, h * place.columns : (h + 1) * place.columns] for h in range(2))
        else:
            piece, which = (i - 4) // 2, i % 2
            at = [(h * PIECES + piece) * place.columns for h in range(2)]
            low, high = (mlp_in[:, which, t : t + place.columns] for t in at)
        low, high = low.astype(BF), high.astype(BF)
        w[i, place.half_rows(core), place.z_columns(0)] = jnp.where(core == 0, low, high)
        theirs[i] = jnp.where(core == 0, high, low)

    def swap_weights(first, count, index):
        there = w.at[pl.ds(first, count), place.half_rows(core), place.z_columns(0)]
        return swap(theirs.at[pl.ds(first, count)], there, index, place.at(core=1))

    def split_rows(src, dst):
        middle, last = SEQ + HALF, 2 * SEQ
        whole = input_grad
        whole[...] = src[...].astype(F32)
        gap = jnp.zeros((FULL - SEQ, src.shape[1]), F32)
        dst[0:FULL, :] = jnp.concatenate((whole[0:SEQ, :], gap)).astype(BF)
        dst[FULL:OWN, :] = jnp.concatenate((whole[SEQ:middle, :], gap)).astype(BF)
        upper = jnp.concatenate((gap[0:1], whole[middle:last, :], gap))
        dst[OWN:ALL, :] = upper.astype(BF)
        dst[ALL:, :] = jnp.concatenate((whole[last:, :], gap)).astype(BF)

    for i in range(4):
        split_weights(i)
    pl.semaphore_wait(barrier, 7 + place.chips - 1)
    copy_weights = swap_weights(0, 4, 0)
    loads[0].wait()
    copy_weights.wait()
    gather_to(0)
    for i in range(4, ITEMS):
        split_weights(i)
    copy_weights = swap_weights(4, ITEMS - 4, 1)
    loads[1].wait()
    split_rows(inputs, out_got)
    copy_weights.wait()
    gather_to(2)
    waits, swaps, done = [], [], 0

    def send_cot(chunk):
        cot_waits.append(send_rows(grad_got, cot, chunk, 7 + chunk))

    parts = ((0, 1), (2, 3), (4, 5), (6,))
    for n, part in enumerate(parts):
        for chunk in part:
            waits.append(send_rows(out_got, x, chunk, chunk))
        pump()
        for chunk in part:
            swaps.append(waits[chunk]())
        if n == 1:
            loads[2].wait()
            split_rows(cotangent, grad_got)
        if n:
            for chunk in parts[n - 1]:
                swaps[chunk].wait()
            while done + 80 <= SECTIONS[chunk][0] + SECTIONS[chunk][1]:
                norm_rows(done)
                done += 80
    cot_waits, cot_swaps = [], []
    send_cot(0)
    swaps[6].wait()

    def norm_more(start):
        norm_rows(pl.multiple_of(done + start, 16))

    tiles(ALL - done, 80, norm_more)
    pump()
    gather_item(KEY)
    project(QUERY, q, head_bias(4))
    project(KEY, k, None)
    pump()
    send_cot(1)
    gather_item(VALUE)
    project(VALUE, v, head_bias(5))
    for pair in range(4):
        attend(pair)
        if pair % 2:
            pump()
        if pair < 3:
            cot_swaps.append(cot_waits[pair]())
            send_cot(2 + pair)

    gather_item(OUT)
    def out_other(start):
        rows = other_rows(224, start)
        box[pl.ds(start, 224), :] = dot(mixed[rows, :], w[OUT], (1, 1)).astype(BF)

    tiles(CORE_ROWS, 224, out_other)
    copy_attn = swap(box, got_half, 6, place.at(core=1))

    def out_own(start):
        rows = own_rows(224, start)
        value = dot(mixed[rows, :], w[OUT], (1, 1))
        res[pl.ds(start, 224), :] = value + x[rows, :].astype(F32) + vec[6:7, :]

    tiles(CORE_ROWS, 224, out_own)
    copy_attn.wait()

    def norm_two(start):
        rows = pl.ds(start, 32)
        value = res[rows, :] + got_half[rows, :].astype(F32)
        res[rows, :] = value
        normed, _ = normalize(value)
        ln_two[own_rows(32, start), :] = (normed * vec[2:3, :] + vec[3:4, :]).astype(BF)

    tiles(CORE_ROWS, 32, norm_two)
    mine_two = ln_two.at[own_rows(CORE_ROWS), :]
    copy_two = swap(mine_two, mine_two, 7, place.at(core=1))
    pump()
    cot_swaps.append(cot_waits[3]())
    cot_swaps.append(cot_waits[4]())
    gather_item(5)
    for copy in cot_swaps:
        copy.wait()
    copy_two.wait()

    up_sums[...] = jnp.zeros_like(up_sums)

    def mlp_piece(piece, hook):
        up, down = 4 + 2 * piece, 5 + 2 * piece
        gather_item(down)
        bias = up_bias(piece)

        def rows_part(start):
            rows = pl.ds(start, CORE_ROWS)
            pre[...] = dot(ln_two[rows, :], w[up], (1, 0))
            gh[...] = dot(cot[rows, :], w[down], (1, 0))

            def activate(at):
                inside = pl.ds(at, 32)
                u = pre[inside, :] + bias
                cdf, slope = gelu_parts(u)
                grad = (gh[inside, :] * (cdf + slope)).astype(BF)
                hid[pl.ds(start + at, 32), :] = (u * cdf).astype(BF)
                gp[pl.ds(start + at, 32), :] = grad
                up_sums[piece] += row_sum(grad.astype(F32))

            tiles(CORE_ROWS, 32, activate)
            out = dot(hid[rows, :], w[down], (1, 1))
            two = dot(gp[rows, :], w[up], (1, 1))
            if piece:
                acc_out[rows, :] += out
                acc_two[rows, :] += two
            else:
                acc_out[rows, :] = out
                acc_two[rows, :] = two

        tiles(OWN, CORE_ROWS, rows_part)
        hook()

        def up_rows(start):
            rows = pl.ds(start, 256)
            w[up, rows, :] = dot(ln_two[:, rows], gp[...], (0, 0)).astype(BF)
            w[down, rows, :] = dot(cot[:, rows], hid[...], (0, 0)).astype(BF)

        tiles(width, 256, up_rows)

    def nothing():
        pass

    def gather_near(left):
        return lambda: gather_to(gather_last - left)

    mlp_piece(0, gather_near(4))
    gather_near(3)()
    advance(0)
    mlp_piece(1, gather_near(2))
    advance(1)
    mlp_piece(2, lambda: None)
    gather_near(1)()
    advance(2, 0)
    mlp_piece(3, lambda: None)
    advance(3, 1, 0)

    def send_half(acc, start):
        box[pl.ds(start, 64), :] = acc[other_rows(64, start), :].astype(BF)

    tiles(CORE_ROWS, 64, lambda start: send_half(acc_two, start))
    copy_two = swap(box, got_half, 8, place.at(core=1))
    sums[...] = jnp.zeros_like(sums)
    copy_two.wait()

    def back_two(start):
        rows, held = pl.ds(start, 32), own_rows(32, start)
        normed, inv_std = normalize(res[rows, :])
        grad = acc_two[held, :] + got_half[rows, :].astype(F32)
        grad_out = cot[held, :].astype(F32)
        acc_two[held, :] = grad_out + normalize_back(grad * vec[2:3, :], normed, inv_std)
        sums[2] += row_sum(grad * normed)
        sums[3] += row_sum(grad)
        sums[6] += row_sum(acc_two[held, :])
        sums[7] += row_sum(grad_out)
        ln_two[held, :] = acc_two[held, :].astype(BF)

    tiles(CORE_ROWS, 32, back_two)
    advance(4, 0)
    mine_two = ln_two.at[own_rows(CORE_ROWS), :]
    copy_grad = swap(mine_two, mine_two, 9, place.at(core=1))
    tiles(CORE_ROWS, 64, lambda start: send_half(acc_out, start))
    copy_out = swap(box, got_out, 10, place.at(core=1))
    copy_grad.wait()

    def grad_heads(start):
        rows = pl.ds(start, CORE_ROWS)
        hid[rows, :] = dot(ln_two[rows, :], w[OUT], (1, 0)).astype(BF)

    tiles(OWN, CORE_ROWS, grad_heads)
    advance(5, 2, 1, 0)

    def weight_grad(item, left, size, right):
        def body(start):
            rows = pl.ds(start, 256)
            w[item, rows, :] = dot(left[0:size, rows], right[0:size, :], (0, 0)).astype(BF)

        tiles(width, 256, body)

    pump()

    def got_rows(got, slot):
        return got.at[pl.ds(pl.multiple_of(slot * CORE_ROWS, CORE_ROWS), CORE_ROWS), :]

    class SendRows:
        def __init__(self, got, index):
            self.got, self.index = got, index
            self.slot = 2 * z_low + core

        def start(self, first, size):
            rows = pl.ds(first, size)
            there = pl.ds(pl.multiple_of(self.slot * CORE_ROWS + first, 16), size)
            for f in range(4):
                src, dst = box.at[rows, f * 256 : (f + 1) * 256], self.got.at[there, :]
                recv = ms_recv.at[self.index + 4 + self.slot]
                here = stay & (z == f)

                @pl.when(here)
                def _():
                    pltpu.make_async_copy(src, dst, recv).start()

                @pl.when(jnp.logical_not(here))
                def _():
                    remote(src, dst, ms_send.at[self.index + f], recv, (2 * place.chip + z_high, f))

        def wait(self):
            for f in range(4):
                src = box.at[:, f * 256 : (f + 1) * 256]

                @pl.when(jnp.logical_not(stay & (z == f)))
                def _():
                    pltpu.make_async_remote_copy(
                        src_ref=src, dst_ref=got_rows(self.got, 0), send_sem=ms_send.at[self.index + f],
                        recv_sem=ms_recv.at[self.index + 4], device_id=place.at(core=1), device_id_type=MESH,
                    ).wait_send()

            for slot in range(4):
                recv = ms_recv.at[self.index + 4 + slot]
                pltpu.make_async_copy(box.at[:, 0:256], got_rows(self.got, slot), recv).wait()

    def output_rows(start):
        rows = pl.ds(start, 32)
        value = res[rows, :] + acc_out[own_rows(32, start), :] + got_out[rows, :].astype(F32)
        box[rows, :] = (value + vec[7:8, :]).astype(BF)

    def join_rows(got, dst):
        split, shared = SEQ - CORE_ROWS, FULL - CORE_ROWS
        last = 2 * SEQ
        even, odd = CORE_ROWS, 3 * CORE_ROWS
        dst[0:CORE_ROWS, :] = got[0:CORE_ROWS, :].astype(F32)
        dst[CORE_ROWS:SEQ, :] = got[even : even + split, :].astype(F32)
        dst[SEQ : SEQ + HALF, :] = got[even + shared : even + shared + HALF, :].astype(F32)
        dst[SEQ + HALF : last, :] = got[odd + shared : odd + shared + HALF, :].astype(F32)[1:, :]
        dst[last : last + CORE_ROWS, :] = got[2 * CORE_ROWS : odd, :].astype(F32)
        dst[last + CORE_ROWS :, :] = got[odd : odd + split, :].astype(F32)

    copy_out.wait()
    tiles(CORE_ROWS, 32, output_rows)
    send_output = SendRows(out_got, 16)
    send_output.start(0, 112)
    weight_grad(OUT, ln_two, OWN, mixed)
    for pair in range(4):
        attend_back(pair)
        advance(*((3, 1, 0), (6, 2, 1), (7, 4, 3, 2), (8, 5, 1))[pair])
        if pair < 3:
            send_output.start(112 * (pair + 1), 112)
    def one_part(rows, size):
        value = dot(k[rows, :], w[KEY], (1, 1)) + dot(v[rows, :], w[VALUE], (1, 1))
        return value + dot(q[rows, :], w[QUERY], (1, 1))

    rest = got_pair.at[0]
    rest_rows = slice(0, PART)

    def rest_copy():
        return pltpu.make_async_remote_copy(
            src_ref=rest, dst_ref=got_rest, send_sem=ms_send.at[12], recv_sem=ms_recv.at[12],
            device_id=place.at(core=1), device_id_type=MESH,
        )

    def pair_copy():
        return pltpu.make_async_remote_copy(
            src_ref=rest, dst_ref=got_pair.at[1], send_sem=ms_send.at[13], recv_sem=ms_recv.at[13],
            device_id=place.at(z=1), device_id_type=MESH,
        )

    def one_other(start):
        cot[pl.ds(start, 224), :] = one_part(other_rows(224, start), 224).astype(BF)

    tiles(CORE_ROWS, 224, one_other)
    copy_one = swap(cot.at[0:CORE_ROWS, :], got_half, 11, place.at(core=1))
    value = dot(k[OWN:, :], w[KEY], (1, 1)) + dot(v[OWN:, :], w[VALUE], (1, 1))
    acc_out[0:PART, :] = value
    rest[...] = acc_out[rest_rows, :].astype(BF)

    @pl.when(core == 0)
    def _():
        rest_copy().start()

    weight_grad(4, ln_one, ALL, v)
    advance(4, 6, 9)

    @pl.when(core == 0)
    def _():
        rest_copy().wait_send()

    @pl.when(core == 1)
    def _():
        rest_copy().wait_recv()
        rest[...] = (acc_out[rest_rows, :] + got_rest[...].astype(F32)).astype(BF)
        pair_copy().start()

    weight_grad(5, ln_one, ALL, k)
    advance(3, 2)

    def one_own(start):
        rows = own_rows(224, start)
        res[pl.ds(start, 224), :] = one_part(rows, 224)

    tiles(CORE_ROWS, 224, one_own)
    send_output.wait()
    copy_one.wait()

    @pl.when(core == 1)
    def _():
        pair_copy().wait()
        start = FULL - CORE_ROWS
        res[start:, :] = res[start:, :] + got_pair[1].astype(F32)

    def back_one(start):
        rows, held = pl.ds(start, 32), own_rows(32, start)
        normed, inv_std = normalize(x[held, :].astype(F32))
        grad = res[rows, :] + got_half[rows, :].astype(F32)
        sums[0] += row_sum(grad * normed)
        sums[1] += row_sum(grad)
        value = acc_two[held, :] + normalize_back(grad * vec[0:1, :], normed, inv_std)
        box[rows, :] = value.astype(BF)

    tiles(CORE_ROWS, 32, back_one)
    send_grad = SendRows(grad_got, 24)
    send_grad.start(0, 112)
    advance(2, 5, 7, 10)
    assert stage[:3] == [6] * 3
    weight_grad(6, ln_one, OWN, q)
    send_grad.start(112, 112)
    advance(6, 8, 11)

    def sum_heads(ref, size):
        def body(start):
            value = ref[pl.ds(start, 16), :].astype(F32)
            pre[0:8, :] += row_sum(value)

        pre[0:8, :] = jnp.zeros((8, pre.shape[1]), F32)
        tiles(size, 16, body)
        return jnp.sum(pre[0:8, :], axis=0, keepdims=True)

    def spread(value):
        left = jnp.where(core == 0, value, 0.0)
        right = jnp.where(core == 0, 0.0, value)
        size = place.columns
        parts = []
        for i in range(place.zs):
            parts += [left[:, i * size : (i + 1) * size], right[:, i * size : (i + 1) * size]]
        return jnp.concatenate(parts, axis=1)

    vec_part[...] = jnp.zeros_like(vec_part)
    ups = [jnp.sum(up_sums[piece], axis=0, keepdims=True) for piece in range(PIECES)]
    for i in range(place.zs):
        size = place.columns
        row = jnp.concatenate([up[:, i * size : (i + 1) * size] for up in ups], axis=1)
        left, right = jnp.where(core == 0, row, 0.0), jnp.where(core == 0, 0.0, row)
        vec_part[8 + i : 9 + i, :] = jnp.concatenate((left, right), axis=1)
    vec_part[4:5, :] = spread(sum_heads(q, OWN))
    vec_part[5:6, :] = spread(sum_heads(v, ALL))
    for row in (0, 1, 2, 3, 6, 7):
        vec_part[row : row + 1, :] = jnp.sum(sums[row], axis=0, keepdims=True)
    vec_steps = sum_steps(place, vec_part, vec_sum, vec_slots, vs_send, vs_recv)
    next(vec_steps)
    join_rows(out_got, input_grad)
    output[...] = input_grad[...].astype(BF)
    advance(7, 9, 3, 4, 5)
    send_grad.start(224, 112)
    advance(6, 8, 10, 3, 4, 5, 7)
    send_grad.start(336, 112)
    advance(6, 9, 11, 4, 8, 5, 7, 6, 10, 9, 8, 11, 7)
    next(vec_steps)
    advance(10, 9, 8, 11)
    next(vec_steps)
    advance(10, 9, 11, 10, 11)
    assert stage == [6] * ITEMS
    for _ in vec_steps:
        pass
    norm_sum[...] = jnp.zeros_like(norm_sum)

    @pl.loop(0, ITEMS)
    def _(i):
        value = fin[i].astype(F32)
        norm_sum[...] += jnp.sum((value * value).reshape(-1, 8, value.shape[-1]), axis=0)

    norm_steps = sum_quickly(place, norm_sum, norm_slots, ns_send, ns_recv)
    next(norm_steps)
    send_grad.wait()
    join_rows(grad_got, input_grad)
    for i in range(ITEMS):
        for h in range(2):
            value = fin[i, h].astype(F32)
            if i < 4:
                attn_grad[:, i, h * place.columns : (h + 1) * place.columns] = value
            else:
                at = (h * PIECES + (i - 4) // 2) * place.columns
                mlp_grad[:, i % 2, at : at + place.columns] = value
    for _ in norm_steps:
        pass
    rows = lax.broadcasted_iota(jnp.int32, vec_sum.shape, 0)
    held = jnp.where(rows < vec.shape[0], vec_sum[...], 0.0)
    total = jnp.sum(norm_sum[...], keepdims=True) + jnp.sum(held * held, keepdims=True)
    norm_out[...] = jnp.broadcast_to(jnp.sqrt(total), norm_out.shape)


def run_layer(attn_weights, mlp_weights, inputs, cotangent, vec):
    width = vec.shape[1]
    rows, columns = attn_weights.shape[0], attn_weights.shape[2] // 2
    token_count, features = inputs.shape
    chips = lax.axis_size("dp") // 2
    bits = chips.bit_length() - 1
    heads = 4 * columns
    slots = 8 + chips
    block = 2 * rows
    whole = pl.BlockSpec(memory_space=pltpu.VMEM)
    hbm = pl.BlockSpec(memory_space=pl.ANY)

    def buf(*shape, dtype=BF):
        return pltpu.VMEM(shape, dtype)

    gather_copies = 3 + bits + chips - 1
    scatter_copies = 2 * (chips - 1) + 4
    scratch = [
        buf(ITEMS, width, heads),
        buf(ITEMS, rows, columns),
        buf(token_count, features),
        buf(token_count, features),
        buf(ITEMS, 2, rows, columns),
        buf(4 * CORE_ROWS, features),
        buf(4 * CORE_ROWS, features),
        buf(8, 128, dtype=F32),
        buf(ALL, width),
        buf(ALL, width),
        buf(ALL, heads),
        buf(ALL, heads),
        buf(ALL, heads),
        buf(OWN, heads),
        buf(OWN, heads, dtype=F32),
        buf(OWN, width),
        buf(OWN, width),
        buf(OWN, width, dtype=F32),
        buf(OWN, width, dtype=F32),
        buf(CORE_ROWS, width, dtype=F32),
        buf(CORE_ROWS, heads, dtype=F32),
        buf(CORE_ROWS, heads, dtype=F32),
        buf(OWN, heads),
        buf(OWN, heads),
        buf(CORE_ROWS, width),
        buf(CORE_ROWS, width),
        buf(CORE_ROWS, width),
        buf(PART, width),
        buf(2, PART, width),
        buf(SLOTS, (chips - 1) * block, heads),
        buf(COLUMN_SLOTS, block, 3 * columns),
        buf(8, 8, width, dtype=F32),
        buf(PIECES, 8, heads, dtype=F32),
        buf(16, width, dtype=F32),
        buf(8 + chips, 16, width // 8, dtype=F32),
        buf(slots, 8, 128, dtype=F32),
        pltpu.SemaphoreType.DMA((GATHER_SLOTS, gather_copies)),
        pltpu.SemaphoreType.DMA((GATHER_SLOTS, gather_copies)),
        pltpu.SemaphoreType.DMA((COLUMN_SLOTS, scatter_copies)),
        pltpu.SemaphoreType.DMA((COLUMN_SLOTS, scatter_copies)),
        pltpu.SemaphoreType.DMA((12, 3)),
        pltpu.SemaphoreType.DMA((12, 3)),
        pltpu.SemaphoreType.DMA((32,)),
        pltpu.SemaphoreType.DMA((32,)),
        pltpu.SemaphoreType.DMA((14 + chips,)),
        pltpu.SemaphoreType.DMA((14 + chips,)),
        pltpu.SemaphoreType.DMA((slots,)),
        pltpu.SemaphoreType.DMA((slots,)),
    ]
    return pl.pallas_call(
        layer_kernel,
        in_specs=[whole, hbm, hbm, hbm, whole],
        out_specs=[whole] * 6,
        out_shape=[
            jax.ShapeDtypeStruct((token_count, features), BF),
            jax.ShapeDtypeStruct((token_count, features), F32),
            jax.ShapeDtypeStruct(attn_weights.shape, F32),
            jax.ShapeDtypeStruct(mlp_weights.shape, F32),
            jax.ShapeDtypeStruct((16, width), F32),
            jax.ShapeDtypeStruct((8, 128), F32),
        ],
        scratch_shapes=scratch,
        compiler_params=pltpu.CompilerParams(
            collective_id=0, has_side_effects=True, vmem_limit_bytes=VMEM_LIMIT
        ),
        name="layer",
    )(attn_weights, mlp_weights, inputs, cotangent, vec)


def adam_step(weight, grad, mean, square, rate, decay):
    next_mean = beta_one * mean + (1.0 - beta_one) * grad
    next_square = beta_two * square + (1.0 - beta_two) * grad * grad
    mean_hat = next_mean / (1.0 - beta_one**STEP)
    square_hat = next_square / (1.0 - beta_two**STEP)
    updated = weight - rate * (mean_hat / (jnp.sqrt(square_hat) + adam_eps) + decay * weight)
    return (updated, next_mean, next_square)


def adam_kernel(clip_limit, norm, *refs):
    ins, outs = refs[:12], refs[13:]
    factor = jnp.minimum(1.0, clip_limit / (norm[0:1, 0:1] + norm_eps))
    refs[12][0, 0] = jnp.max(norm[...])
    for n in range(2):
        weight, grad, mean, square = ins[4 * n : 4 * n + 4]
        for i in range(weight.shape[1]):
            results = adam_step(
                weight[:, i, :], factor * grad[:, i, :], mean[:, i, :], square[:, i, :],
                rate_matrix, decay_matrix,
            )
            for out, value in zip(outs[3 * n : 3 * n + 3], results):
                out[:, i, :] = value
    weight, grad, mean, square = ins[8:]
    held = slice(0, weight.shape[0])
    results = adam_step(weight[...], factor * grad[held, :], mean[...], square[...], rate_vector, 0.0)
    for out, value in zip(outs[6:], results):
        out[...] = value


def run_adam(clip_limit, norm, attn, mlp, vector):
    parts = 4
    rows = attn[0].shape[0] // parts

    def block(value):
        return pl.BlockSpec((rows,) + value.shape[1:], lambda i: (i, 0, 0))

    def whole(value):
        return pl.BlockSpec(value.shape, lambda i: (0, 0))

    groups = (attn, mlp, vector)
    specs = [block, block, whole]
    return pl.pallas_call(
        functools.partial(adam_kernel, clip_limit),
        grid=(parts,),
        in_specs=[whole(norm)] + [spec(a) for spec, group in zip(specs, groups) for a in group],
        out_specs=[pl.BlockSpec(memory_space=pltpu.SMEM)]
        + [spec(group[0]) for spec, group in zip(specs, groups) for _ in range(3)],
        out_shape=[jax.ShapeDtypeStruct((1, 1), F32)]
        + [jax.ShapeDtypeStruct(group[0].shape, F32) for group in groups for _ in range(3)],
        compiler_params=pltpu.CompilerParams(vmem_limit_bytes=VMEM_LIMIT),
        name="adam",
    )(norm, *attn, *mlp, *vector)


def shards(
    inputs,
    cotangent,
    attn_weights,
    mlp_weights,
    vectors,
    attn_mean,
    mlp_mean,
    vector_mean,
    attn_square,
    mlp_square,
    vector_square,
):
    tensor_count = lax.axis_size("tensor")
    data_count = lax.axis_size("dp")
    token_count, feature_local = inputs.shape
    width = feature_local * tensor_count
    hidden_cols = mlp_weights.shape[2]
    assert tensor_count == 4 and token_count == 3 * SEQ
    assert attn_weights.shape[2] * PIECES == hidden_cols == width

    output, input_grad, attn_grad, mlp_grad, vec_sum, norm_out = run_layer(
        attn_weights, mlp_weights, inputs, cotangent, vectors
    )
    clip_limit = clip_ratio * math.sqrt(width * hidden_cols * tensor_count * token_count * data_count)
    attn = (attn_weights, attn_grad, attn_mean, attn_square)
    mlp = (mlp_weights, mlp_grad, mlp_mean, mlp_square)
    vector = (vectors, vec_sum, vector_mean, vector_square)
    grad_norm, *results = run_adam(clip_limit, norm_out, attn, mlp, vector)
    updated_attn, next_attn_mean, next_attn_square = results[:3]
    updated_mlp, next_mlp_mean, next_mlp_square = results[3:6]
    updated_vectors, next_vector_mean, next_vector_square = results[6:]
    grad_norm = grad_norm.reshape(())
    return (
        output,
        input_grad,
        grad_norm,
        updated_attn,
        updated_mlp,
        updated_vectors,
        next_attn_mean,
        next_mlp_mean,
        next_vector_mean,
        next_attn_square,
        next_mlp_square,
        next_vector_square,
    )


def solution(mesh):
    rows = P("dp", "tensor")
    weight = P("dp", None, "tensor")
    return jax.shard_map(
        shards,
        mesh=mesh,
        in_specs=(rows, rows) + (weight, weight, P()) * 3,
        out_specs=(rows, rows, P()) + (weight, weight, P()) * 3,
        check_vma=False,
    )
```

```python
import functools
import math

import jax
import jax.numpy as jnp
from jax import lax
from jax.experimental import pallas as pl
from jax.experimental.pallas import tpu as pltpu
from jax.sharding import PartitionSpec as P

HD = 64
SEQ = 577
STEP = 10

beta_one = 0.9
beta_two = 0.999
rate_matrix = 0.1
rate_vector = 0.5
decay_matrix = 0.1
adam_eps = 1e-08
norm_eps = 1e-06
clip_ratio = 0.025

BF = jnp.bfloat16
F32 = jnp.float32

FULL = 592
PART = 304
HALF = SEQ // 2 + 1
OWN = FULL + PART
ALL = OWN + PART
CORE_ROWS = OWN // 2
PIECES = 4
ITEMS = 4 + 2 * PIECES
VMEM_LIMIT = 64 * 2**20
SLOTS = 6
COLUMN_SLOTS = 8
GATHER_SLOTS = 8
QUERY, KEY, VALUE, OUT = range(4)
MESH = pl.DeviceIdType.MESH


def dot(left, right, dims):
    return lax.dot_general(left, right, ((dims[:1], dims[1:]), ((), ())), preferred_element_type=F32)


def xor(index, mask):
    out = index
    bit = 1
    while bit <= mask:
        if mask & bit:
            out = out + bit * (1 - 2 * ((index // bit) % 2))
        bit *= 2
    return out


def normalize(rows_in):
    center = rows_in - jnp.mean(rows_in, axis=-1, keepdims=True)
    inv_std = lax.rsqrt(jnp.mean(center * center, axis=-1, keepdims=True) + norm_eps)
    return center * inv_std, inv_std


def normalize_back(scaled, normed, inv_std):
    return inv_std * (
        scaled
        - jnp.mean(scaled, axis=-1, keepdims=True)
        - normed * jnp.mean(scaled * normed, axis=-1, keepdims=True)
    )


def gelu_parts(u):
    a = jnp.abs(u)
    t = 1.0 / (1.0 + (0.3275911 / math.sqrt(2.0)) * a)
    e = jnp.exp(-0.5 * u * u)
    poly = t * (
        0.254829592 + t * (-0.284496736 + t * (1.421413741 + t * (-1.453152027 + t * 1.061405429)))
    )
    tail = 0.5 * poly * e
    phi_big = jnp.where(u >= 0, 1.0 - tail, tail)
    return phi_big, u * e * (1.0 / math.sqrt(2.0 * math.pi))


class Place:
    def __init__(self, rows, columns):
        self.dp = lax.axis_index("dp")
        self.z = lax.axis_index("tensor")
        self.core = self.dp % 2
        self.chip = self.dp // 2
        self.chips = lax.axis_size("dp") // 2
        self.zs = lax.axis_size("tensor")
        self.core_rows = rows
        self.rows = 2 * rows
        self.columns = columns
        count = self.chips.bit_length() - 1
        fast = [1 << i for i in range((count + 1) // 2)]
        slow = [1 << i for i in range((count + 1) // 2, count)]
        self.orders = (fast + slow, slow + fast)
        self.z_bits = [1 << i for i in range(self.zs.bit_length() - 1)]

    def at(self, core=0, chip=0, z=0):
        return (xor(self.dp, core + 2 * chip), xor(self.z, z))

    def chip_rows(self, mask, count=1):
        return pl.ds(pl.multiple_of(xor(self.chip, mask) * self.rows, self.rows), count * self.rows)

    def z_columns(self, mask):
        return pl.ds(pl.multiple_of(xor(self.z, mask) * self.columns, self.columns), self.columns)

    def half_rows(self, core):
        start = self.chip * self.rows + core * self.core_rows
        return pl.ds(pl.multiple_of(start, self.core_rows), self.core_rows)


def remote(src, dst, send, recv, device):
    copy = pltpu.make_async_remote_copy(
        src_ref=src, dst_ref=dst, send_sem=send, recv_sem=recv, device_id=device, device_id_type=MESH
    )
    copy.start()
    return copy


def gather_steps(place, weight, send_sem, recv_sem):
    used = [0]

    def send(rows, columns, device):
        ref = weight.at[rows, columns]
        k = used[0]
        used[0] += 1
        return remote(ref, ref, send_sem.at[k], recv_sem.at[k], device)

    have = [0]
    for bit in reversed(place.z_bits):
        copies = [send(place.chip_rows(0), place.z_columns(m), place.at(z=bit)) for m in have]
        yield
        for copy in copies:
            copy.wait()
        have = have + [m ^ bit for m in have]
    width = place.zs * place.columns
    parts = (slice(0, width // 2), slice(width // 2, width))
    haves = [[0], [0]]
    for step in range(len(place.orders[0])):
        copies = []
        for i, columns in enumerate(parts):
            bit = place.orders[i][step]
            masks = sorted(haves[i])
            count = len(masks)
            if masks == list(range(count)):
                start = place.chip // count * count
                rows = pl.ds(pl.multiple_of(start * place.rows, place.rows), count * place.rows)
                copies.append(send(rows, columns, place.at(chip=bit)))
            else:
                for m in masks:
                    copies.append(send(place.chip_rows(m), columns, place.at(chip=bit)))
            haves[i] = masks + [m ^ bit for m in masks]
        yield
        for copy in copies:
            copy.wait()


def add_block(ref, rows, columns, other):
    ref[rows, columns] = (ref[rows, columns].astype(F32) + other.astype(F32)).astype(BF)


def scatter_steps(place, weight, by_rows, by_columns, final, send_sem, recv_sem):
    used = [0]

    def send(src, dst, device):
        k = used[0]
        used[0] += 1
        return remote(src, dst, send_sem.at[k], recv_sem.at[k], device)

    width = place.zs * place.columns
    parts = (slice(0, width // 2), slice(width // 2, width))
    haves = [list(range(place.chips))] * 2
    base = 0
    for step in reversed(range(len(place.orders[0]))):
        copies, adds = [], []
        bits = [order[step] for order in place.orders]
        haves = [[m for m in have if not m & bit] for have, bit in zip(haves, bits)]
        for slot in range(len(haves[0])):
            there = pl.ds(base + slot * place.rows, place.rows)
            for columns, bit, have in zip(parts, bits, haves):
                m = have[slot]
                src = weight.at[place.chip_rows(m ^ bit), columns]
                copies.append(send(src, by_rows.at[there, columns], place.at(chip=bit)))
                adds.append((place.chip_rows(m), columns, there))
        base += len(haves[0]) * place.rows
        yield
        for copy in copies:
            copy.wait()
        for rows, columns, there in adds:
            add_block(weight, rows, columns, by_rows[there, columns])
    have = list(range(place.zs))
    base = 0
    for bit in place.z_bits:
        keep = [m for m in have if not m & bit]
        copies, adds = [], []
        for slot, m in enumerate(keep):
            there = pl.ds(base + slot * place.columns, place.columns)
            src = weight.at[place.chip_rows(0), place.z_columns(m ^ bit)]
            copies.append(send(src, by_columns.at[:, there], place.at(z=bit)))
            adds.append((m, there))
        base += len(keep) * place.columns
        have = keep
        yield
        for copy in copies:
            copy.wait()
        for m, there in adds:
            add_block(weight, place.chip_rows(0), place.z_columns(m), by_columns[:, there])
    other = weight.at[place.half_rows(1 - place.core), place.z_columns(0)]
    copy = send(other, final.at[place.core], place.at(core=1))
    final[pl.ds(place.core, 1)] = weight[place.half_rows(place.core), place.z_columns(0)][None]
    yield
    copy.wait()


def sum_steps(place, value, result, parts, send_sem, recv_sem):
    size = value.shape[1] // 8
    here = place.core * place.zs + place.z
    used = [0]

    def columns(index):
        return pl.ds(pl.multiple_of(index * size, size), size)

    def send(src, dst, partner):
        k = used[0]
        used[0] += 1
        return remote(src, dst, send_sem.at[k], recv_sem.at[k], partner)

    others = [(k // 4, k % 4) for k in range(1, 8)]
    parts[pl.ds(here, 1)] = value[:, columns(here)][None]
    copies = []
    for c, m in others:
        there = xor(place.core, c) * place.zs + xor(place.z, m)
        copies.append(send(value.at[:, columns(there)], parts.at[here], place.at(core=c, z=m)))
    yield
    for copy in copies:
        copy.wait()
    total = parts[0]
    for k in range(1, 8):
        total = total + parts[k]
    parts[pl.ds(8 + place.chip, 1)] = total[None]
    mine = parts.at[8 + place.chip]
    copies = [send(mine, mine, place.at(chip=k)) for k in range(1, place.chips)]
    yield
    for copy in copies:
        copy.wait()
    total = parts[8]
    for k in range(1, place.chips):
        total = total + parts[8 + k]
    result[:, columns(here)] = total
    mine = result.at[:, columns(here)]
    copies = [send(mine, mine, place.at(core=c, z=m)) for c, m in others]
    yield
    for copy in copies:
        copy.wait()


def sum_quickly(place, value, slots, send_sem, recv_sem):
    others = [place.at(core=k // 4, z=k % 4) for k in range(1, 8)]
    column = (place.core * place.zs + place.z, 8, 0, others)
    chips = (place.chip, place.chips, 8, [place.at(chip=k) for k in range(1, place.chips)])
    for here, count, base, partners in (column, chips):
        slots[pl.ds(base + here, 1)] = value[...][None]
        slot = slots.at[base + here]
        copies = [
            remote(slot, slot, send_sem.at[base + k], recv_sem.at[base + k], partner)
            for k, partner in enumerate(partners)
        ]
        yield
        for copy in copies:
            copy.wait()
        total = slots[base]
        for k in range(1, count):
            total = total + slots[base + k]
        value[...] = total


def layer_kernel(
    attn_in, mlp_hbm, inputs_hbm, cot_hbm, vec,
    output, input_grad, attn_grad, mlp_grad, vec_sum, norm_out,
    w, theirs, inputs, cotangent, fin, out_got, grad_got, norm_sum, x, ln_one, q, k, v, mixed, lse, cot, ln_two, acc_out, acc_two, res, pre, gh, hid, gp,
    box, got_half, got_out, got_rest, got_pair, by_rows, by_columns,
    sums, up_sums, vec_part, vec_slots, norm_slots,
    ag_send, ag_recv, rs_send, rs_recv, xs_send, xs_recv, ms_send, ms_recv, vs_send, vs_recv, ns_send, ns_recv,
):
    width = x.shape[1]
    place = Place(fin.shape[2], fin.shape[3])
    core, z = place.core, place.z
    z_low = z % 2
    z_high = z // 2


    mlp_in = mlp_grad
    barrier = pltpu.get_barrier_semaphore()
    for c in range(2):
        for m in range(4):
            if c or m:
                pl.semaphore_signal(barrier, inc=1, device_id=place.at(core=c, z=m), device_id_type=MESH)
    for chip in range(1, place.chips):
        pl.semaphore_signal(barrier, inc=1, device_id=place.at(chip=chip), device_id_type=MESH)
    loads = [
        pltpu.make_async_copy(src, dst, ms_send.at[24 + i])
        for i, (src, dst) in enumerate(((mlp_hbm, mlp_in), (inputs_hbm, inputs), (cot_hbm, cotangent)))
    ]
    for load in loads:
        load.start()

    gathers = [
        gather_steps(place, w.at[i], ag_send.at[i % GATHER_SLOTS], ag_recv.at[i % GATHER_SLOTS])
        for i in range(ITEMS)
    ]
    steps = len(place.orders[0])
    offsets = [0, 1] + [2 + 2 * s for s in range(steps + 1)]
    entry_tick = [max(i // 2, i - 2) for i in range(ITEMS)]
    gather_events = sorted(
        (entry_tick[i] + offset, -s, i) for i in range(ITEMS) for s, offset in enumerate(offsets)
    )
    gather_last = gather_events[-1][0]

    def gather_item(item):
        gather_to(entry_tick[item] + offsets[-1])

    tick = {"gather": 0}

    def gather_to(now):
        while gather_events and gather_events[0][0] <= now:
            next(gathers[gather_events.pop(0)[2]], None)
        tick["gather"] = max(tick["gather"], now)

    scatter_order = [(i, i) for i in range(4, ITEMS)]
    scatter_order += [(OUT, OUT), (VALUE, 4), (KEY, 5), (QUERY, 6)]
    scatters = [
        scatter_steps(
            place, w.at[slot], by_rows.at[n % SLOTS], by_columns.at[n % COLUMN_SLOTS], fin.at[i],
            rs_send.at[n % COLUMN_SLOTS], rs_recv.at[n % COLUMN_SLOTS],
        )
        for n, (i, slot) in enumerate(scatter_order)
    ]
    stage = [0] * ITEMS

    def advance(*which):
        for n in which:
            for _ in range(steps - 1 if stage[n] == 2 else 1):
                next(scatters[n], None)
            stage[n] += 1

    def pump():
        if tick["gather"] < gather_last:
            gather_to(tick["gather"] + 1)

    def swap(src, dst, index, device):
        return remote(src, dst, ms_send.at[index], ms_recv.at[index], device)

    stay = core == z_high

    SECTIONS = []
    odd_full = FULL + 2 * PART
    for start, size, even, odd in (
        (0, FULL, 0, odd_full), (FULL, PART, FULL, OWN), (OWN, PART, OWN, FULL)
    ):
        cuts = (208, 192, 192) if size == FULL else (160, 144)
        for cut in cuts:
            SECTIONS.append((start, cut, even, odd))
            start, even, odd = start + cut, even + cut, odd + cut

    def send_rows(src, dst, section, chunk):
        start, size, even, odd = SECTIONS[section]
        columns = pl.ds(pl.multiple_of(z * src.shape[1], src.shape[1]), src.shape[1])
        rows = pl.ds(start, size)
        there = dst.at[rows, columns]
        first = pl.multiple_of(even + z_low * (odd - even), 16)
        second = pl.multiple_of(odd + z_low * (even - odd), 16)
        src_same, src_cross = src.at[pl.ds(first, size), :], src.at[pl.ds(second, size), :]
        target = (2 * place.chip + z_high, 2 * core + z_low)
        other = (2 * place.chip + z_high, 2 * core + 1 - z_low)

        @pl.when(stay)
        def _():
            pltpu.make_async_copy(src_same, there, xs_recv.at[chunk, 0]).start()

        @pl.when(jnp.logical_not(stay))
        def _():
            remote(src_same, there, xs_send.at[chunk, 0], xs_recv.at[chunk, 0], target)

        copy = remote(src_cross, there, xs_send.at[chunk, 1], xs_recv.at[chunk, 1], other)

        def wait():
            whole = pltpu.make_async_remote_copy(
                src_ref=src_same, dst_ref=there, send_sem=xs_send.at[chunk, 0],
                recv_sem=xs_recv.at[chunk, 0], device_id=other, device_id_type=MESH,
            )

            @pl.when(jnp.logical_not(stay))
            def _():
                whole.wait_send()

            whole.wait_recv()
            copy.wait()

            half = width // 2
            here = dst.at[rows, pl.ds(pl.multiple_of(core * half, half), half)]
            return remote(here, here, xs_send.at[chunk, 2], xs_recv.at[chunk, 2], place.at(core=1))

        return wait

    def own_rows(size, start=0):
        return pl.ds(pl.multiple_of(core * CORE_ROWS + start, 16), size)

    def other_rows(size, start=0):
        return pl.ds(pl.multiple_of((1 - core) * CORE_ROWS + start, 16), size)

    def tiles(total, size, body):
        @pl.loop(0, total // size)
        def _(t):
            body(pl.multiple_of(t * size, size))

    def norm_rows(start):
        rows = pl.ds(start, 80)
        normed, _ = normalize(x[rows, :].astype(F32))
        ln_one[rows, :] = (normed * vec[0:1, :] + vec[1:2, :]).astype(BF)

    def head_bias(row):
        size = place.columns
        parts = []
        for i in range(place.zs):
            low = vec[row : row + 1, 2 * i * size : (2 * i + 1) * size]
            high = vec[row : row + 1, (2 * i + 1) * size : (2 * i + 2) * size]
            parts.append(jnp.where(core == 0, low, high))
        return jnp.concatenate(parts, axis=1)

    def up_bias(piece):
        size = place.columns
        parts = []
        for i in range(place.zs):
            low = vec[8 + i : 9 + i, piece * size : (piece + 1) * size]
            high = vec[8 + i : 9 + i, (PIECES + piece) * size : (PIECES + piece + 1) * size]
            parts.append(jnp.where(core == 0, low, high))
        return jnp.concatenate(parts, axis=1)

    def project(item, dst, bias):
        def body(start):
            rows = pl.ds(start, 240)
            value = dot(ln_one[rows, :], w[item], (1, 0))
            if bias is not None:
                value = value + bias
            dst[rows, :] = value.astype(BF)

        tiles(ALL, 240, body)

    IMAGES = ((0, FULL, FULL), (FULL, PART, 2 * PART))

    def masked(q_in, k_in, low):
        scores = dot(q_in, k_in, (1, 1)) * HD**-0.5
        col = lax.broadcasted_iota(jnp.int32, scores.shape, 1)
        if low:
            inside = jnp.where(col < PART, col, col - PART)
            good = (inside < HALF) & (col != PART * (1 - z_low))
        else:
            good = col < SEQ
        return jnp.where(good, scores, -1e30)

    def attend(pair):
        lanes = pl.ds(pl.multiple_of(pair * 2 * HD, 2 * HD), 2 * HD)
        for low, size, keys in IMAGES:
            q_in, k_in, v_in = q[low : low + size, lanes], k[low : low + keys, lanes], v[low : low + keys, lanes]
            outs, logs = [], []
            for head in range(2):
                cut = slice(head * HD, (head + 1) * HD)
                scores = masked(q_in[:, cut], k_in[:, cut], low)
                peaks = jnp.max(scores, axis=-1, keepdims=True)
                exponent = jnp.exp(scores - peaks)
                totals = jnp.sum(exponent, axis=-1, keepdims=True)
                probs = (exponent * (1.0 / totals)).astype(BF)
                outs.append(dot(probs, v_in[:, cut], (1, 0)))
                logs.append(jnp.broadcast_to(peaks + jnp.log(totals), (size, HD)))
            mixed[low : low + size, lanes] = jnp.concatenate(outs, axis=1).astype(BF)
            lse[low : low + size, lanes] = jnp.concatenate(logs, axis=1)

    def attend_back(pair):
        lanes = pl.ds(pl.multiple_of(pair * 2 * HD, 2 * HD), 2 * HD)
        scale = HD**-0.5
        for low, size, keys in IMAGES:
            q_in, k_in, v_in = q[low : low + size, lanes], k[low : low + keys, lanes], v[low : low + keys, lanes]
            do_in, o_in = hid[low : low + size, lanes], mixed[low : low + size, lanes]
            logs = lse[low : low + size, lanes]
            dqs, dks, dvs = [], [], []
            for head in range(2):
                cut = slice(head * HD, (head + 1) * HD)
                do = do_in[:, cut]
                scores = masked(q_in[:, cut], k_in[:, cut], low)
                probs = jnp.exp(scores - logs[:, head * HD : head * HD + 1])
                grad_probs = dot(do, v_in[:, cut], (1, 1))
                delta = jnp.sum(do.astype(F32) * o_in[:, cut].astype(F32), axis=-1, keepdims=True)
                ds = (probs * (grad_probs - delta)).astype(BF)
                dqs.append(dot(ds, k_in[:, cut], (1, 0)) * scale)
                dks.append(dot(ds, q_in[:, cut], (0, 0)) * scale)
                dvs.append(dot(probs.astype(BF), do, (0, 0)))
            q[low : low + size, lanes] = jnp.concatenate(dqs, axis=1).astype(BF)
            k[low : low + keys, lanes] = jnp.concatenate(dks, axis=1).astype(BF)
            v[low : low + keys, lanes] = jnp.concatenate(dvs, axis=1).astype(BF)

    def row_sum(value):
        return jnp.sum(value.reshape(-1, 8, value.shape[-1]), axis=0)

    def split_weights(i):
        if i < 4:
            low, high = (attn_in[:, i, h * place.columns : (h + 1) * place.columns] for h in range(2))
        else:
            piece, which = (i - 4) // 2, i % 2
            at = [(h * PIECES + piece) * place.columns for h in range(2)]
            low, high = (mlp_in[:, which, t : t + place.columns] for t in at)
        low, high = low.astype(BF), high.astype(BF)
        w[i, place.half_rows(core), place.z_columns(0)] = jnp.where(core == 0, low, high)
        theirs[i] = jnp.where(core == 0, high, low)

    def swap_weights(first, count, index):
        there = w.at[pl.ds(first, count), place.half_rows(core), place.z_columns(0)]
        return swap(theirs.at[pl.ds(first, count)], there, index, place.at(core=1))

    def split_rows(src, dst):
        middle, last = SEQ + HALF, 2 * SEQ
        whole = input_grad
        whole[...] = src[...].astype(F32)
        gap = jnp.zeros((FULL - SEQ, src.shape[1]), F32)
        dst[0:FULL, :] = jnp.concatenate((whole[0:SEQ, :], gap)).astype(BF)
        dst[FULL:OWN, :] = jnp.concatenate((whole[SEQ:middle, :], gap)).astype(BF)
        upper = jnp.concatenate((gap[0:1], whole[middle:last, :], gap))
        dst[OWN:ALL, :] = upper.astype(BF)
        dst[ALL:, :] = jnp.concatenate((whole[last:, :], gap)).astype(BF)

    for i in range(4):
        split_weights(i)
    pl.semaphore_wait(barrier, 7 + place.chips - 1)
    copy_weights = swap_weights(0, 4, 0)
    loads[0].wait()
    copy_weights.wait()
    gather_to(0)
    for i in range(4, ITEMS):
        split_weights(i)
    copy_weights = swap_weights(4, ITEMS - 4, 1)
    loads[1].wait()
    split_rows(inputs, out_got)
    copy_weights.wait()
    gather_to(2)
    waits, swaps, done = [], [], 0

    def send_cot(chunk):
        cot_waits.append(send_rows(grad_got, cot, chunk, 7 + chunk))

    parts = ((0, 1), (2, 3), (4, 5), (6,))
    for n, part in enumerate(parts):
        for chunk in part:
            waits.append(send_rows(out_got, x, chunk, chunk))
        pump()
        for chunk in part:
            swaps.append(waits[chunk]())
        if n == 1:
            loads[2].wait()
            split_rows(cotangent, grad_got)
        if n:
            for chunk in parts[n - 1]:
                swaps[chunk].wait()
            while done + 80 <= SECTIONS[chunk][0] + SECTIONS[chunk][1]:
                norm_rows(done)
                done += 80
    cot_waits, cot_swaps = [], []
    send_cot(0)
    swaps[6].wait()

    def norm_more(start):
        norm_rows(pl.multiple_of(done + start, 16))

    tiles(ALL - done, 80, norm_more)
    pump()
    gather_item(KEY)
    project(QUERY, q, head_bias(4))
    project(KEY, k, None)
    pump()
    send_cot(1)
    gather_item(VALUE)
    project(VALUE, v, head_bias(5))
    for pair in range(4):
        attend(pair)
        if pair % 2:
            pump()
        if pair < 3:
            cot_swaps.append(cot_waits[pair]())
            send_cot(2 + pair)

    gather_item(OUT)
    def out_other(start):
        rows = other_rows(224, start)
        box[pl.ds(start, 224), :] = dot(mixed[rows, :], w[OUT], (1, 1)).astype(BF)

    tiles(CORE_ROWS, 224, out_other)
    copy_attn = swap(box, got_half, 6, place.at(core=1))

    def out_own(start):
        rows = own_rows(224, start)
        value = dot(mixed[rows, :], w[OUT], (1, 1))
        res[pl.ds(start, 224), :] = value + x[rows, :].astype(F32) + vec[6:7, :]

    tiles(CORE_ROWS, 224, out_own)
    copy_attn.wait()

    def norm_two(start):
        rows = pl.ds(start, 32)
        value = res[rows, :] + got_half[rows, :].astype(F32)
        res[rows, :] = value
        normed, _ = normalize(value)
        ln_two[own_rows(32, start), :] = (normed * vec[2:3, :] + vec[3:4, :]).astype(BF)

    tiles(CORE_ROWS, 32, norm_two)
    mine_two = ln_two.at[own_rows(CORE_ROWS), :]
    copy_two = swap(mine_two, mine_two, 7, place.at(core=1))
    pump()
    cot_swaps.append(cot_waits[3]())
    cot_swaps.append(cot_waits[4]())
    gather_item(5)
    for copy in cot_swaps:
        copy.wait()
    copy_two.wait()

    up_sums[...] = jnp.zeros_like(up_sums)

    def mlp_piece(piece, hook):
        up, down = 4 + 2 * piece, 5 + 2 * piece
        gather_item(down)
        bias = up_bias(piece)

        def rows_part(start):
            rows = pl.ds(start, CORE_ROWS)
            pre[...] = dot(ln_two[rows, :], w[up], (1, 0))
            gh[...] = dot(cot[rows, :], w[down], (1, 0))

            def activate(at):
                inside = pl.ds(at, 32)
                u = pre[inside, :] + bias
                cdf, slope = gelu_parts(u)
                grad = (gh[inside, :] * (cdf + slope)).astype(BF)
                hid[pl.ds(start + at, 32), :] = (u * cdf).astype(BF)
                gp[pl.ds(start + at, 32), :] = grad
                up_sums[piece] += row_sum(grad.astype(F32))

            tiles(CORE_ROWS, 32, activate)
            out = dot(hid[rows, :], w[down], (1, 1))
            two = dot(gp[rows, :], w[up], (1, 1))
            if piece:
                acc_out[rows, :] += out
                acc_two[rows, :] += two
            else:
                acc_out[rows, :] = out
                acc_two[rows, :] = two

        tiles(OWN, CORE_ROWS, rows_part)
        hook()

        def up_rows(start):
            rows = pl.ds(start, 256)
            w[up, rows, :] = dot(ln_two[:, rows], gp[...], (0, 0)).astype(BF)
            w[down, rows, :] = dot(cot[:, rows], hid[...], (0, 0)).astype(BF)

        tiles(width, 256, up_rows)

    def nothing():
        pass

    def gather_near(left):
        return lambda: gather_to(gather_last - left)

    mlp_piece(0, gather_near(4))
    gather_near(3)()
    advance(0)
    mlp_piece(1, gather_near(2))
    advance(1)
    mlp_piece(2, lambda: None)
    gather_near(1)()
    advance(2, 0)
    mlp_piece(3, lambda: None)
    advance(3, 1, 0)

    def send_half(acc, start):
        box[pl.ds(start, 64), :] = acc[other_rows(64, start), :].astype(BF)

    tiles(CORE_ROWS, 64, lambda start: send_half(acc_two, start))
    copy_two = swap(box, got_half, 8, place.at(core=1))
    sums[...] = jnp.zeros_like(sums)
    copy_two.wait()

    def back_two(start):
        rows, held = pl.ds(start, 32), own_rows(32, start)
        normed, inv_std = normalize(res[rows, :])
        grad = acc_two[held, :] + got_half[rows, :].astype(F32)
        grad_out = cot[held, :].astype(F32)
        acc_two[held, :] = grad_out + normalize_back(grad * vec[2:3, :], normed, inv_std)
        sums[2] += row_sum(grad * normed)
        sums[3] += row_sum(grad)
        sums[6] += row_sum(acc_two[held, :])
        sums[7] += row_sum(grad_out)
        ln_two[held, :] = acc_two[held, :].astype(BF)

    tiles(CORE_ROWS, 32, back_two)
    advance(4, 0)
    mine_two = ln_two.at[own_rows(CORE_ROWS), :]
    copy_grad = swap(mine_two, mine_two, 9, place.at(core=1))
    tiles(CORE_ROWS, 64, lambda start: send_half(acc_out, start))
    copy_out = swap(box, got_out, 10, place.at(core=1))
    copy_grad.wait()

    def grad_heads(start):
        rows = pl.ds(start, CORE_ROWS)
        hid[rows, :] = dot(ln_two[rows, :], w[OUT], (1, 0)).astype(BF)

    tiles(OWN, CORE_ROWS, grad_heads)
    advance(5, 2, 1, 0)

    def weight_grad(item, left, size, right):
        def body(start):
            rows = pl.ds(start, 256)
            w[item, rows, :] = dot(left[0:size, rows], right[0:size, :], (0, 0)).astype(BF)

        tiles(width, 256, body)

    pump()

    def got_rows(got, slot):
        return got.at[pl.ds(pl.multiple_of(slot * CORE_ROWS, CORE_ROWS), CORE_ROWS), :]

    class SendRows:
        def __init__(self, got, index):
            self.got, self.index = got, index
            self.slot = 2 * z_low + core

        def start(self, first, size):
            rows = pl.ds(first, size)
            there = pl.ds(pl.multiple_of(self.slot * CORE_ROWS + first, 16), size)
            for f in range(4):
                src, dst = box.at[rows, f * 256 : (f + 1) * 256], self.got.at[there, :]
                recv = ms_recv.at[self.index + 4 + self.slot]
                here = stay & (z == f)

                @pl.when(here)
                def _():
                    pltpu.make_async_copy(src, dst, recv).start()

                @pl.when(jnp.logical_not(here))
                def _():
                    remote(src, dst, ms_send.at[self.index + f], recv, (2 * place.chip + z_high, f))

        def wait(self):
            for f in range(4):
                src = box.at[:, f * 256 : (f + 1) * 256]

                @pl.when(jnp.logical_not(stay & (z == f)))
                def _():
                    pltpu.make_async_remote_copy(
                        src_ref=src, dst_ref=got_rows(self.got, 0), send_sem=ms_send.at[self.index + f],
                        recv_sem=ms_recv.at[self.index + 4], device_id=place.at(core=1), device_id_type=MESH,
                    ).wait_send()

            for slot in range(4):
                recv = ms_recv.at[self.index + 4 + slot]
                pltpu.make_async_copy(box.at[:, 0:256], got_rows(self.got, slot), recv).wait()

    def output_rows(start):
        rows = pl.ds(start, 32)
        value = res[rows, :] + acc_out[own_rows(32, start), :] + got_out[rows, :].astype(F32)
        box[rows, :] = (value + vec[7:8, :]).astype(BF)

    def join_rows(got, dst):
        split, shared = SEQ - CORE_ROWS, FULL - CORE_ROWS
        last = 2 * SEQ
        even, odd = CORE_ROWS, 3 * CORE_ROWS
        dst[0:CORE_ROWS, :] = got[0:CORE_ROWS, :].astype(F32)
        dst[CORE_ROWS:SEQ, :] = got[even : even + split, :].astype(F32)
        dst[SEQ : SEQ + HALF, :] = got[even + shared : even + shared + HALF, :].astype(F32)
        dst[SEQ + HALF : last, :] = got[odd + shared : odd + shared + HALF, :].astype(F32)[1:, :]
        dst[last : last + CORE_ROWS, :] = got[2 * CORE_ROWS : odd, :].astype(F32)
        dst[last + CORE_ROWS :, :] = got[odd : odd + split, :].astype(F32)

    copy_out.wait()
    tiles(CORE_ROWS, 32, output_rows)
    send_output = SendRows(out_got, 16)
    send_output.start(0, 112)
    weight_grad(OUT, ln_two, OWN, mixed)
    for pair in range(4):
        attend_back(pair)
        advance(*((3, 1, 0), (6, 2, 1), (7, 4, 3, 2), (8, 5, 1))[pair])
        if pair < 3:
            send_output.start(112 * (pair + 1), 112)
    def one_part(rows, size):
        value = dot(k[rows, :], w[KEY], (1, 1)) + dot(v[rows, :], w[VALUE], (1, 1))
        return value + dot(q[rows, :], w[QUERY], (1, 1))

    rest = got_pair.at[0]
    rest_rows = slice(0, PART)

    def rest_copy():
        return pltpu.make_async_remote_copy(
            src_ref=rest, dst_ref=got_rest, send_sem=ms_send.at[12], recv_sem=ms_recv.at[12],
            device_id=place.at(core=1), device_id_type=MESH,
        )

    def pair_copy():
        return pltpu.make_async_remote_copy(
            src_ref=rest, dst_ref=got_pair.at[1], send_sem=ms_send.at[13], recv_sem=ms_recv.at[13],
            device_id=place.at(z=1), device_id_type=MESH,
        )

    def one_other(start):
        cot[pl.ds(start, 224), :] = one_part(other_rows(224, start), 224).astype(BF)

    tiles(CORE_ROWS, 224, one_other)
    copy_one = swap(cot.at[0:CORE_ROWS, :], got_half, 11, place.at(core=1))
    value = dot(k[OWN:, :], w[KEY], (1, 1)) + dot(v[OWN:, :], w[VALUE], (1, 1))
    acc_out[0:PART, :] = value
    rest[...] = acc_out[rest_rows, :].astype(BF)

    @pl.when(core == 0)
    def _():
        rest_copy().start()

    weight_grad(4, ln_one, ALL, v)
    advance(4, 6, 9)

    @pl.when(core == 0)
    def _():
        rest_copy().wait_send()

    @pl.when(core == 1)
    def _():
        rest_copy().wait_recv()
        rest[...] = (acc_out[rest_rows, :] + got_rest[...].astype(F32)).astype(BF)
        pair_copy().start()

    weight_grad(5, ln_one, ALL, k)
    advance(3, 2)

    def one_own(start):
        rows = own_rows(224, start)
        res[pl.ds(start, 224), :] = one_part(rows, 224)

    tiles(CORE_ROWS, 224, one_own)
    send_output.wait()
    copy_one.wait()

    @pl.when(core == 1)
    def _():
        pair_copy().wait()
        start = FULL - CORE_ROWS
        res[start:, :] = res[start:, :] + got_pair[1].astype(F32)

    def back_one(start):
        rows, held = pl.ds(start, 32), own_rows(32, start)
        normed, inv_std = normalize(x[held, :].astype(F32))
        grad = res[rows, :] + got_half[rows, :].astype(F32)
        sums[0] += row_sum(grad * normed)
        sums[1] += row_sum(grad)
        value = acc_two[held, :] + normalize_back(grad * vec[0:1, :], normed, inv_std)
        box[rows, :] = value.astype(BF)

    tiles(CORE_ROWS, 32, back_one)
    send_grad = SendRows(grad_got, 24)
    send_grad.start(0, 112)
    advance(2, 5, 7, 10)
    assert stage[:3] == [6] * 3
    weight_grad(6, ln_one, OWN, q)
    send_grad.start(112, 112)
    advance(6, 8, 11)

    def sum_heads(ref, size):
        def body(start):
            value = ref[pl.ds(start, 16), :].astype(F32)
            pre[0:8, :] += row_sum(value)

        pre[0:8, :] = jnp.zeros((8, pre.shape[1]), F32)
        tiles(size, 16, body)
        return jnp.sum(pre[0:8, :], axis=0, keepdims=True)

    def spread(value):
        left = jnp.where(core == 0, value, 0.0)
        right = jnp.where(core == 0, 0.0, value)
        size = place.columns
        parts = []
        for i in range(place.zs):
            parts += [left[:, i * size : (i + 1) * size], right[:, i * size : (i + 1) * size]]
        return jnp.concatenate(parts, axis=1)

    vec_part[...] = jnp.zeros_like(vec_part)
    ups = [jnp.sum(up_sums[piece], axis=0, keepdims=True) for piece in range(PIECES)]
    for i in range(place.zs):
        size = place.columns
        row = jnp.concatenate([up[:, i * size : (i + 1) * size] for up in ups], axis=1)
        left, right = jnp.where(core == 0, row, 0.0), jnp.where(core == 0, 0.0, row)
        vec_part[8 + i : 9 + i, :] = jnp.concatenate((left, right), axis=1)
    vec_part[4:5, :] = spread(sum_heads(q, OWN))
    vec_part[5:6, :] = spread(sum_heads(v, ALL))
    for row in (0, 1, 2, 3, 6, 7):
        vec_part[row : row + 1, :] = jnp.sum(sums[row], axis=0, keepdims=True)
    vec_steps = sum_steps(place, vec_part, vec_sum, vec_slots, vs_send, vs_recv)
    next(vec_steps)
    join_rows(out_got, input_grad)
    output[...] = input_grad[...].astype(BF)
    advance(7, 9, 3, 4, 5)
    send_grad.start(224, 112)
    advance(6, 8, 10, 3, 4, 5, 7)
    send_grad.start(336, 112)
    advance(6, 9, 11, 4, 8, 5, 7, 6, 10, 9, 8, 11, 7)
    next(vec_steps)
    advance(10, 9, 8, 11)
    next(vec_steps)
    advance(10, 9, 11, 10, 11)
    assert stage == [6] * ITEMS
    for _ in vec_steps:
        pass
    norm_sum[...] = jnp.zeros_like(norm_sum)

    @pl.loop(0, ITEMS)
    def _(i):
        value = fin[i].astype(F32)
        norm_sum[...] += jnp.sum((value * value).reshape(-1, 8, value.shape[-1]), axis=0)

    norm_steps = sum_quickly(place, norm_sum, norm_slots, ns_send, ns_recv)
    next(norm_steps)
    send_grad.wait()
    join_rows(grad_got, input_grad)
    for i in range(ITEMS):
        for h in range(2):
            value = fin[i, h].astype(F32)
            if i < 4:
                attn_grad[:, i, h * place.columns : (h + 1) * place.columns] = value
            else:
                at = (h * PIECES + (i - 4) // 2) * place.columns
                mlp_grad[:, i % 2, at : at + place.columns] = value
    for _ in norm_steps:
        pass
    rows = lax.broadcasted_iota(jnp.int32, vec_sum.shape, 0)
    held = jnp.where(rows < vec.shape[0], vec_sum[...], 0.0)
    total = jnp.sum(norm_sum[...], keepdims=True) + jnp.sum(held * held, keepdims=True)
    norm_out[...] = jnp.broadcast_to(jnp.sqrt(total), norm_out.shape)


def run_layer(attn_weights, mlp_weights, inputs, cotangent, vec):
    width = vec.shape[1]
    rows, columns = attn_weights.shape[0], attn_weights.shape[2] // 2
    token_count, features = inputs.shape
    chips = lax.axis_size("dp") // 2
    bits = chips.bit_length() - 1
    heads = 4 * columns
    slots = 8 + chips
    block = 2 * rows
    whole = pl.BlockSpec(memory_space=pltpu.VMEM)
    hbm = pl.BlockSpec(memory_space=pl.ANY)

    def buf(*shape, dtype=BF):
        return pltpu.VMEM(shape, dtype)

    gather_copies = 3 + bits + chips - 1
    scatter_copies = 2 * (chips - 1) + 4
    scratch = [
        buf(ITEMS, width, heads),
        buf(ITEMS, rows, columns),
        buf(token_count, features),
        buf(token_count, features),
        buf(ITEMS, 2, rows, columns),
        buf(4 * CORE_ROWS, features),
        buf(4 * CORE_ROWS, features),
        buf(8, 128, dtype=F32),
        buf(ALL, width),
        buf(ALL, width),
        buf(ALL, heads),
        buf(ALL, heads),
        buf(ALL, heads),
        buf(OWN, heads),
        buf(OWN, heads, dtype=F32),
        buf(OWN, width),
        buf(OWN, width),
        buf(OWN, width, dtype=F32),
        buf(OWN, width, dtype=F32),
        buf(CORE_ROWS, width, dtype=F32),
        buf(CORE_ROWS, heads, dtype=F32),
        buf(CORE_ROWS, heads, dtype=F32),
        buf(OWN, heads),
        buf(OWN, heads),
        buf(CORE_ROWS, width),
        buf(CORE_ROWS, width),
        buf(CORE_ROWS, width),
        buf(PART, width),
        buf(2, PART, width),
        buf(SLOTS, (chips - 1) * block, heads),
        buf(COLUMN_SLOTS, block, 3 * columns),
        buf(8, 8, width, dtype=F32),
        buf(PIECES, 8, heads, dtype=F32),
        buf(16, width, dtype=F32),
        buf(8 + chips, 16, width // 8, dtype=F32),
        buf(slots, 8, 128, dtype=F32),
        pltpu.SemaphoreType.DMA((GATHER_SLOTS, gather_copies)),
        pltpu.SemaphoreType.DMA((GATHER_SLOTS, gather_copies)),
        pltpu.SemaphoreType.DMA((COLUMN_SLOTS, scatter_copies)),
        pltpu.SemaphoreType.DMA((COLUMN_SLOTS, scatter_copies)),
        pltpu.SemaphoreType.DMA((12, 3)),
        pltpu.SemaphoreType.DMA((12, 3)),
        pltpu.SemaphoreType.DMA((32,)),
        pltpu.SemaphoreType.DMA((32,)),
        pltpu.SemaphoreType.DMA((14 + chips,)),
        pltpu.SemaphoreType.DMA((14 + chips,)),
        pltpu.SemaphoreType.DMA((slots,)),
        pltpu.SemaphoreType.DMA((slots,)),
    ]
    return pl.pallas_call(
        layer_kernel,
        in_specs=[whole, hbm, hbm, hbm, whole],
        out_specs=[whole] * 6,
        out_shape=[
            jax.ShapeDtypeStruct((token_count, features), BF),
            jax.ShapeDtypeStruct((token_count, features), F32),
            jax.ShapeDtypeStruct(attn_weights.shape, F32),
            jax.ShapeDtypeStruct(mlp_weights.shape, F32),
            jax.ShapeDtypeStruct((16, width), F32),
            jax.ShapeDtypeStruct((8, 128), F32),
        ],
        scratch_shapes=scratch,
        compiler_params=pltpu.CompilerParams(
            collective_id=0, has_side_effects=True, vmem_limit_bytes=VMEM_LIMIT
        ),
        name="layer",
    )(attn_weights, mlp_weights, inputs, cotangent, vec)


def adam_step(weight, grad, mean, square, rate, decay):
    next_mean = beta_one * mean + (1.0 - beta_one) * grad
    next_square = beta_two * square + (1.0 - beta_two) * grad * grad
    mean_hat = next_mean / (1.0 - beta_one**STEP)
    square_hat = next_square / (1.0 - beta_two**STEP)
    updated = weight - rate * (mean_hat / (jnp.sqrt(square_hat) + adam_eps) + decay * weight)
    return (updated, next_mean, next_square)


def adam_kernel(clip_limit, norm, *refs):
    kept, refs = refs[:2], refs[2:]
    ins, outs, given = refs[:12], refs[13:22], refs[22:]
    for src, dst in zip(kept, given):
        dst[...] = src[...]
    factor = jnp.minimum(1.0, clip_limit / (norm[0:1, 0:1] + norm_eps))
    refs[12][0, 0] = jnp.max(norm[...])
    for n in range(2):
        weight, grad, mean, square = ins[4 * n : 4 * n + 4]
        for i in range(weight.shape[1]):
            results = adam_step(
                weight[:, i, :], factor * grad[:, i, :], mean[:, i, :], square[:, i, :],
                rate_matrix, decay_matrix,
            )
            for out, value in zip(outs[3 * n : 3 * n + 3], results):
                out[:, i, :] = value
    weight, grad, mean, square = ins[8:]
    held = slice(0, weight.shape[0])
    results = adam_step(weight[...], factor * grad[held, :], mean[...], square[...], rate_vector, 0.0)
    for out, value in zip(outs[6:], results):
        out[...] = value


def run_adam(clip_limit, norm, kept, attn, mlp, vector):
    parts = 4
    rows = attn[0].shape[0] // parts

    def block(value):
        return pl.BlockSpec((rows,) + value.shape[1:], lambda i: (i, 0, 0))

    def whole(value):
        return pl.BlockSpec(value.shape, lambda i: (0, 0))

    token = pl.BlockSpec((CORE_ROWS, kept[0].shape[1]), lambda i: (i, 0))
    groups = (attn, mlp, vector)
    specs = [block, block, whole]
    return pl.pallas_call(
        functools.partial(adam_kernel, clip_limit),
        grid=(parts,),
        in_specs=[whole(norm), token, token] + [spec(a) for spec, group in zip(specs, groups) for a in group],
        out_specs=[pl.BlockSpec(memory_space=pltpu.SMEM)]
        + [spec(group[0]) for spec, group in zip(specs, groups) for _ in range(3)]
        + [token, token],
        out_shape=[jax.ShapeDtypeStruct((1, 1), F32)]
        + [jax.ShapeDtypeStruct(group[0].shape, F32) for group in groups for _ in range(3)]
        + [jax.ShapeDtypeStruct(a.shape, a.dtype) for a in kept],
        compiler_params=pltpu.CompilerParams(vmem_limit_bytes=VMEM_LIMIT),
        name="adam",
    )(norm, *kept, *attn, *mlp, *vector)


def shards(
    inputs,
    cotangent,
    attn_weights,
    mlp_weights,
    vectors,
    attn_mean,
    mlp_mean,
    vector_mean,
    attn_square,
    mlp_square,
    vector_square,
):
    tensor_count = lax.axis_size("tensor")
    data_count = lax.axis_size("dp")
    token_count, feature_local = inputs.shape
    width = feature_local * tensor_count
    hidden_cols = mlp_weights.shape[2]
    assert tensor_count == 4 and token_count == 3 * SEQ
    assert attn_weights.shape[2] * PIECES == hidden_cols == width

    output, input_grad, attn_grad, mlp_grad, vec_sum, norm_out = run_layer(
        attn_weights, mlp_weights, inputs, cotangent, vectors
    )
    clip_limit = clip_ratio * math.sqrt(width * hidden_cols * tensor_count * token_count * data_count)
    attn = (attn_weights, attn_grad, attn_mean, attn_square)
    mlp = (mlp_weights, mlp_grad, mlp_mean, mlp_square)
    vector = (vectors, vec_sum, vector_mean, vector_square)
    grad_norm, *results = run_adam(clip_limit, norm_out, (output, input_grad), attn, mlp, vector)
    updated_attn, next_attn_mean, next_attn_square = results[:3]
    updated_mlp, next_mlp_mean, next_mlp_square = results[3:6]
    updated_vectors, next_vector_mean, next_vector_square, output, input_grad = results[6:]
    grad_norm = grad_norm.reshape(())
    return (
        output,
        input_grad,
        grad_norm,
        updated_attn,
        updated_mlp,
        updated_vectors,
        next_attn_mean,
        next_mlp_mean,
        next_vector_mean,
        next_attn_square,
        next_mlp_square,
        next_vector_square,
    )


def solution(mesh):
    rows = P("dp", "tensor")
    weight = P("dp", None, "tensor")
    return jax.shard_map(
        shards,
        mesh=mesh,
        in_specs=(rows, rows) + (weight, weight, P()) * 3,
        out_specs=(rows, rows, P()) + (weight, weight, P()) * 3,
        check_vma=False,
    )
```
